512 devices in a mesh: blk: 8 (over y, x_lo), dp: 64 (over z, x_hi, core).
Axes of the slice: x: 4 (x_hi: 2, x_lo: 2; x = x_hi * 2 + x_lo), y: 4, z: 16, core: 2. Of those that a mesh axis runs over, the one named last changes fastest.
Arguments:
- image_features: bfloat16 [65536, 1536], P(('dp', 'blk')), may hold values from -11 to 11
- final_norm_gain: float32 [1536], replicated, may hold values from 0.25 to 1.75
- final_norm_bias: float32 [1536], replicated, may hold values from -3 to 3
- head_weight: bfloat16 [1536, 1536], P('blk'), may hold values from -0.15625 to 0.15625
- text_embed: bfloat16 [65536, 1536], P(('dp', 'blk')), may hold values from -6 to 6
- log_scale: float32 [1], replicated, may hold values from 1.6 to 2.6
- logit_bias: float32 [1], replicated, may hold values from -6 to -2
Outputs:
- grad_image_features: float32 [65536, 1536], P(('dp', 'blk'))
- grad_text: float32 [65536, 1536], P(('dp', 'blk'))
- grad_gain: float32 [1536], replicated
- grad_bias: float32 [1536], replicated
- grad_head: float32 [1536, 1536], P('blk')
The draws below stay inside these ranges and needn't reach their ends.
All inputs are finite; a program needn't handle non-finite values.
Results may differ from the reference program's by a relative error of at most 0.005.
Values may be sent and summed in bfloat16 or wider, within the bound.
No kernel may reach another device: no remote copies, remote signals or barrier semaphores. Data moves between devices by JAX's collectives and lax.ppermute only.
A program may use at most 64 MiB of HBM per device.

```python
import math
import jax
import jax.numpy as jnp
from jax import lax

D = 1536
GROUP = 1024
PAIRS = 65536
N_DP = 64


def draw_image_features(key, part):
    key = jax.random.fold_in(key, 11)
    key_row, key_col, key_noise = jax.random.split(key, 3)
    row_shift = jax.random.uniform(key_row, (PAIRS, 1), jnp.float32, -2.0, 2.0)
    col_scale = jnp.exp(jax.random.uniform(key_col, (1, D), jnp.float32, math.log(0.3), math.log(3.0)))
    noise = jnp.clip(jax.random.normal(key_noise, (PAIRS, D), jnp.float32), -3.0, 3.0)
    return (row_shift + col_scale * noise).astype(jnp.bfloat16)


def levels(rng, extent, cuts, least, largest):
    def one(axis_at, parts):
        steps = jax.random.uniform(jax.random.fold_in(jax.random.fold_in(rng, 6), axis_at), (parts,), jnp.float32, least / len(cuts), largest / len(cuts))
        return jnp.repeat(jnp.exp(steps), extent[axis_at] // parts).reshape((-1,) + (1,) * (len(extent) - axis_at - 1))

    gain = one(*cuts[0])
    for cut in cuts[1:]:
        gain = gain * one(*cut)
    return gain


def bell_draw(rng, dims, scale, most, cuts=(), held_as=jnp.bfloat16):
    entries = scale * jax.random.normal(rng, dims, jnp.float32)
    if cuts:
        entries = entries * levels(rng, dims, cuts, -0.22, 0.18)
    return jnp.clip(entries, -most, most).astype(held_as)


def setup_inputs(seed: int = 0) -> dict:
    key_of = jax.random.split(jax.random.key(seed), 8)
    return {
        "image_features": draw_image_features(jax.random.fold_in(key_of[7], 71), 0),
        "final_norm_gain": jnp.clip(1.0 + 0.15 * jax.random.normal(key_of[1], (D,), jnp.float32), 0.25, 1.75),
        "final_norm_bias": bell_draw(key_of[2], (D,), 0.5, 3.0, (), jnp.float32),
        "head_weight": bell_draw(key_of[3], (D, D), D ** -0.5, 0.15625, ((0, 8),)),
        "text_embed": bell_draw(key_of[4], (PAIRS, D), 1.0, 6.0, ((0, 512),)),
        "log_scale": jnp.clip(jax.random.uniform(key_of[5], (1,), jnp.float32, 1.6, 2.6), 1.6, 2.6),
        "logit_bias": jnp.clip(jax.random.uniform(key_of[6], (1,), jnp.float32, -6.0, -2.0), -6.0, -2.0),
    }


epsilon = 1e-06
loss_scale = 64.0

def reference(image_features, final_norm_gain, final_norm_bias, head_weight, text_embed, log_scale, logit_bias):
    scale = jnp.exp(log_scale[0])
    offset = logit_bias[0]
    eye_group = jnp.eye(GROUP, dtype=jnp.float32)

    def group_step(loop_state, inputs):
        feat_rows, text_rows = inputs
        values = feat_rows.astype(jnp.float32)
        centre = lax.optimization_barrier(jnp.mean(values, axis=1, keepdims=True))
        centered_input = values - centre
        spread = lax.optimization_barrier(jnp.mean(centered_input * centered_input, axis=1, keepdims=True))
        inverse_deviation = lax.rsqrt(spread + epsilon)
        standardized_rows = centered_input * inverse_deviation
        normalized_output = (standardized_rows * final_norm_gain + final_norm_bias).astype(jnp.bfloat16)
        projected = jnp.dot(normalized_output, head_weight, preferred_element_type=jnp.float32)
        inv_proj = lax.rsqrt(lax.optimization_barrier(jnp.sum(projected * projected, axis=1, keepdims=True)) + epsilon)
        image_unit = (projected * inv_proj).astype(jnp.bfloat16)
        text_values = text_rows.astype(jnp.float32)
        inv_text = lax.rsqrt(lax.optimization_barrier(jnp.sum(text_values * text_values, axis=1, keepdims=True)) + epsilon)
        text_unit = (text_values * inv_text).astype(jnp.bfloat16)
        logits = scale * jnp.dot(image_unit, text_unit.T, preferred_element_type=jnp.float32) + offset
        weights = (loss_scale * (jax.nn.sigmoid(logits) - eye_group)).astype(jnp.bfloat16)
        grad_image = scale * jnp.dot(weights, text_unit, preferred_element_type=jnp.float32)
        grad_unit_text = scale * jnp.dot(weights.T, image_unit, preferred_element_type=jnp.float32)
        text_dot = lax.optimization_barrier(jnp.sum(text_values * grad_unit_text, axis=1, keepdims=True))
        grad_text_rows = inv_text * grad_unit_text - inv_text * inv_text * inv_text * text_dot * text_values
        proj_dot = lax.optimization_barrier(jnp.sum(projected * grad_image, axis=1, keepdims=True))
        grad_proj = (inv_proj * grad_image - inv_proj * inv_proj * inv_proj * proj_dot * projected).astype(jnp.bfloat16)
        normalized_gradient = jnp.dot(grad_proj, head_weight.T, preferred_element_type=jnp.float32)
        head_portion = jnp.dot(normalized_output.T, grad_proj, preferred_element_type=jnp.float32)
        scaled_output = normalized_gradient * final_norm_gain
        first_mean_term = lax.optimization_barrier(jnp.mean(scaled_output, axis=1, keepdims=True))
        second_mean_term = lax.optimization_barrier(jnp.mean(scaled_output * standardized_rows, axis=1, keepdims=True))
        feature_gradient_rows = inverse_deviation * (scaled_output - first_mean_term - standardized_rows * second_mean_term)
        head_running_sum, gain_running_sum, bias_running_sum = loop_state
        loop_state = (head_running_sum + head_portion, gain_running_sum + lax.optimization_barrier(jnp.sum(normalized_gradient * standardized_rows, axis=0)), bias_running_sum + lax.optimization_barrier(jnp.sum(normalized_gradient, axis=0)))
        return (loop_state, (feature_gradient_rows, grad_text_rows))
    start_carry = (jnp.zeros((D, D), jnp.float32), jnp.zeros((D,), jnp.float32), jnp.zeros((D,), jnp.float32))
    loop_state, outputs = lax.scan(group_step, start_carry, (image_features.reshape(N_DP, GROUP, D), text_embed.reshape(N_DP, GROUP, D)))
    grad_feats, grad_texts = outputs
    return (grad_feats.reshape(PAIRS, D), grad_texts.reshape(PAIRS, D), loop_state[1] / N_DP, loop_state[2] / N_DP, loop_state[0] / N_DP)
```

```python
import jax
import jax.numpy as jnp
from jax import lax
from jax.sharding import Mesh, PartitionSpec as P

epsilon = 1e-06
loss_scale = 64.0
AXES = ("y", "xl", "z", "xh", "core")
SIZES = (4, 2, 16, 2, 2)
ROWS = ("z", "xh", "core", "y", "xl")
bf16 = jnp.bfloat16
f32 = jnp.float32


def shift(value, axis, steps):
    count = lax.axis_size(axis)
    return lax.ppermute(value, axis, [(i, (i + steps) % count) for i in range(count)])


def shift_x(value, steps):
    def index(place):
        place = place % 4
        return (place % 2) * 2 + place // 2

    return lax.ppermute(value, ("xl", "xh"), [(index(i), index(i + steps)) for i in range(4)])


def swap(value):
    return lax.ppermute(value, ("xl", "core"), [(0, 0), (1, 2), (2, 1), (3, 3)])


def around(value):
    return value, shift(value, "y", -1), shift(value, "y", 1), shift(value, "y", 2)


def halves(flag, first, second, axis):
    return jnp.where(
        flag == 0,
        jnp.concatenate([first, second], axis),
        jnp.concatenate([second, first], axis),
    )


def dot(a, b, da, db):
    return lax.dot_general(a, b, (((da,), (db,)), ((), ())), preferred_element_type=f32)


def split16(value):
    high = value.astype(bf16)
    return high, (value - high.astype(f32)).astype(bf16)


def spread_to(value, axes):
    count = lax.axis_size(axes)
    many = jnp.broadcast_to(value[None], (count,) + value.shape)
    return lax.all_to_all(many, axes, split_axis=0, concat_axis=0, tiled=True)


def gather_weight(head_weight, y, xl, core):
    rows, width = head_weight.shape
    half = width // 2
    part = lax.dynamic_slice(head_weight, (0, core * half), (rows, half))
    blocks = around(part)
    column = jnp.zeros((4, rows, half), bf16)
    for step, block in zip((0, 1, 3, 2), blocks):
        column = lax.dynamic_update_slice(column, block[None], ((y + step) % 4, 0, 0))
    other = jnp.concatenate(
        [shift_x(column[:2], 1), shift_x(column[2:], -1)], 0
    )
    own_half = halves(xl, column, other, 1).reshape(8 * rows, half)
    return halves(core, own_half, shift(own_half, "core", 1), 1)


def local(
    image_features, final_norm_gain, final_norm_bias, head_weight, text_embed, log_scale, logit_bias
):
    y, xl, xh, core = (lax.axis_index(a) for a in ("y", "xl", "xh", "core"))
    scale = jnp.exp(log_scale[0])
    offset = logit_bias[0]
    weight = gather_weight(head_weight, y, xl, core)

    text_values = swap(text_embed).astype(f32)
    values = swap(image_features).astype(f32)
    own, width = values.shape
    inv_text = lax.rsqrt(jnp.sum(text_values * text_values, axis=1, keepdims=True) + epsilon)
    text_unit = (text_values * inv_text).astype(bf16)
    centre = jnp.mean(values, axis=1, keepdims=True)
    centered = values - centre
    spread = jnp.mean(centered * centered, axis=1, keepdims=True)
    inverse_deviation = lax.rsqrt(spread + epsilon)
    xhat = centered * inverse_deviation
    normed_own = (xhat * final_norm_gain + final_norm_bias).astype(bf16)

    text_same = jnp.concatenate(around(text_unit), 0)
    text_other = shift(text_same, "core", 1)
    normed = jnp.concatenate(around(normed_own), 0)
    rows = normed.shape[0]

    projected = dot(normed, weight, 1, 0)
    inv_proj = lax.rsqrt(jnp.sum(projected * projected, axis=1, keepdims=True) + epsilon)
    image_unit = (projected * inv_proj).astype(bf16)

    def weights_of(text_rows, diagonal):
        logits = scale * dot(image_unit, text_rows, 1, 1) + offset
        return (loss_scale * (jax.nn.sigmoid(logits) - diagonal)).astype(bf16)

    weights_same = weights_of(text_same, jnp.eye(rows, dtype=f32))
    weights_other = weights_of(text_other, 0.0)
    grad_image = scale * (dot(weights_same, text_same, 1, 0) + dot(weights_other, text_other, 1, 0))
    proj_dot = jnp.sum(projected * grad_image, axis=1, keepdims=True)
    grad_proj = (
        inv_proj * grad_image - inv_proj * inv_proj * inv_proj * proj_dot * projected
    ).astype(bf16)

    half = width // 2
    block = width // 4
    normed_block = lax.dynamic_slice(normed, (0, y * block), (rows, block))
    mine = lax.dynamic_slice(grad_proj, (0, core * half), (rows, half))
    theirs = lax.dynamic_slice(grad_proj, (0, (1 - core) * half), (rows, half))
    head = dot(normed_block, mine, 0, 0) + shift(
        dot(normed_block, theirs, 0, 0).astype(bf16), "core", 1
    ).astype(f32)
    part = block // 4
    head = head.reshape(4, part, half)
    x_place = xh * 2 + xl

    def for_x(place):
        place = place % 4
        return lax.dynamic_index_in_dim(head, (place % 2) * 2 + place // 2, 0, keepdims=False)

    head_part = for_x(x_place)
    for step in (1, -1, 2):
        head_part = head_part + shift_x(for_x(x_place + step).astype(bf16), step).astype(f32)

    grad_normed = dot(grad_proj[:own], weight, 1, 1)
    scaled = grad_normed * final_norm_gain
    first_mean = jnp.mean(scaled, axis=1, keepdims=True)
    second_mean = jnp.mean(scaled * xhat, axis=1, keepdims=True)
    grad_features = inverse_deviation * (scaled - first_mean - xhat * second_mean)
    vectors = jnp.stack([jnp.sum(grad_normed * xhat, axis=0), jnp.sum(grad_normed, axis=0)], 0)
    vectors = jnp.sum(spread_to(vectors, ("y", "xl", "xh", "core")), axis=0)

    planes = lax.axis_size("z")
    vector_part = 2 * width // planes

    def payload(head_rows, vector):
        high, low = split16(vector)
        rest = jnp.zeros(high.shape[:-1] + (half - 2 * vector_part,), bf16)
        line = jnp.concatenate([high, low, rest], -1)[..., None, :]
        return jnp.concatenate([head_rows.astype(bf16), line], -2)

    def unpack(received):
        line = received[..., -1, :]
        return received[..., :-1, :], line[..., :vector_part] + line[..., vector_part : 2 * vector_part]

    sent = payload(head_part.reshape(planes, part // planes, half), vectors.reshape(planes, vector_part))
    received = lax.all_to_all(sent, "z", split_axis=0, concat_axis=0, tiled=True).astype(f32)
    head_sum, vector_sum = unpack(jnp.sum(received, axis=0))
    head_all, vector_all = unpack(spread_to(payload(head_sum, vector_sum), "z").astype(f32))
    vector_all = vector_all.reshape(2, width) / 64.0

    head_all = head_all.reshape(part, half).astype(bf16)
    head_all = halves(xh, head_all, shift(head_all, "xh", 1), 0)
    head_all = halves(core, head_all, shift(head_all, "core", 1), 1).astype(f32) / 64.0

    grad_unit_text = dot(weights_same[:, :own], image_unit, 0, 0) + shift(
        dot(weights_other[:, :own], image_unit, 0, 0), "core", 1
    )
    grad_unit_text = scale * grad_unit_text
    text_dot = jnp.sum(text_values * grad_unit_text, axis=1, keepdims=True)
    grad_text = inv_text * grad_unit_text - inv_text * inv_text * inv_text * text_dot * text_values

    return (swap(grad_features), swap(grad_text), vector_all[0], vector_all[1], head_all)


def solution(mesh):
    fine = Mesh(mesh.devices.reshape(SIZES), AXES)
    placed = (P(ROWS, None), P(), P(), P(("y", "xl"), None), P(ROWS, None), P(), P())
    return jax.shard_map(
        local,
        mesh=fine,
        in_specs=placed,
        out_specs=(P(ROWS, None), P(ROWS, None), P(), P(), P(("y", "xl"), None)),
        check_vma=False,
    )
```

```python
import jax
import jax.numpy as jnp
from jax import lax
from jax.sharding import Mesh, PartitionSpec as P

epsilon = 1e-06
loss_scale = 64.0
AXES = ("y", "xl", "zh", "zl", "xh", "core")
SIZES = (4, 2, 4, 4, 2, 2)
ROWS = ("zh", "zl", "xh", "core", "y", "xl")
bf16 = jnp.bfloat16
f32 = jnp.float32


def shift(value, axis, steps):
    count = lax.axis_size(axis)
    return lax.ppermute(value, axis, [(i, (i + steps) % count) for i in range(count)])


def shift_x(value, steps):
    def index(place):
        place = place % 4
        return (place % 2) * 2 + place // 2

    return lax.ppermute(value, ("xl", "xh"), [(index(i), index(i + steps)) for i in range(4)])


def swap(value):
    return lax.ppermute(value, ("xl", "core"), [(0, 0), (1, 2), (2, 1), (3, 3)])


def halves(flag, first, second, axis):
    return jnp.where(
        flag == 0,
        jnp.concatenate([first, second], axis),
        jnp.concatenate([second, first], axis),
    )


def dot(a, b, da, db):
    return lax.dot_general(a, b, (((da,), (db,)), ((), ())), preferred_element_type=f32)


def split16(value):
    high = value.astype(bf16)
    return high, (value - high.astype(f32)).astype(bf16)


def spread_to(value, axes):
    count = lax.axis_size(axes)
    many = jnp.broadcast_to(value[None], (count,) + value.shape)
    return lax.all_to_all(many, axes, split_axis=0, concat_axis=0, tiled=True)


def gather_weight(blocks, xl, core):
    other = jnp.concatenate([shift_x(blocks[:2], 1), shift_x(blocks[2:], -1)], 0)
    rows, half = blocks.shape[1:]
    own_half = halves(xl, blocks, other, 1).reshape(8 * rows, half)
    own_half = lax.optimization_barrier(own_half)
    return lax.optimization_barrier(halves(core, own_half, shift(own_half, "core", 1), 1))


def local(
    image_features, final_norm_gain, final_norm_bias, head_weight, text_embed, log_scale, logit_bias
):
    y, xl, xh, core = (lax.axis_index(a) for a in ("y", "xl", "xh", "core"))
    scale = jnp.exp(log_scale[0])
    offset = logit_bias[0]
    own, width = image_features.shape
    half = width // 2
    block = width // 4

    text_rows = swap(text_embed)
    feature_rows = swap(image_features)
    weight_part = lax.dynamic_slice(head_weight, (0, core * half), (head_weight.shape[0], half))
    weight_blocks = spread_to(weight_part, "y")

    text_values = text_rows.astype(f32)
    inv_text = lax.rsqrt(jnp.sum(text_values * text_values, axis=1, keepdims=True) + epsilon)
    text_unit = (text_values * inv_text).astype(bf16)
    text_same = spread_to(text_unit, "y").reshape(4 * own, width)

    values = feature_rows.astype(f32)
    centre = jnp.mean(values, axis=1, keepdims=True)
    centered = values - centre
    spread = jnp.mean(centered * centered, axis=1, keepdims=True)
    inverse_deviation = lax.rsqrt(spread + epsilon)
    xhat = centered * inverse_deviation
    normed_own = (xhat * final_norm_gain + final_norm_bias).astype(bf16)
    weight_blocks, normed_own = lax.optimization_barrier((weight_blocks, normed_own))
    normed = spread_to(normed_own, "y").reshape(4 * own, width)
    rows = normed.shape[0]

    weight = gather_weight(weight_blocks, xl, core)
    text_other = shift(text_same, "core", 1)

    projected = dot(normed, weight, 1, 0)
    inv_proj = lax.rsqrt(jnp.sum(projected * projected, axis=1, keepdims=True) + epsilon)
    image_unit = (projected * inv_proj).astype(bf16)

    def weights_of(text_rows, diagonal):
        logits = scale * dot(image_unit, text_rows, 1, 1) + offset
        return (loss_scale * (jax.nn.sigmoid(logits) - diagonal)).astype(bf16)

    weights_same = weights_of(text_same, jnp.eye(rows, dtype=f32))
    weights_other = weights_of(text_other, 0.0)
    grad_image = scale * (dot(weights_same, text_same, 1, 0) + dot(weights_other, text_other, 1, 0))
    proj_dot = jnp.sum(projected * grad_image, axis=1, keepdims=True)
    grad_proj = (
        inv_proj * grad_image - inv_proj * inv_proj * inv_proj * proj_dot * projected
    ).astype(bf16)

    normed_block = lax.dynamic_slice(normed, (0, y * block), (rows, block))
    mine = lax.dynamic_slice(grad_proj, (0, core * half), (rows, half))
    theirs = lax.dynamic_slice(grad_proj, (0, (1 - core) * half), (rows, half))
    sent = dot(normed_block, theirs, 0, 0).astype(bf16)
    mine, sent = lax.optimization_barrier((mine, sent))
    head = dot(normed_block, mine, 0, 0) + shift(sent, "core", 1).astype(f32)
    part = block // 4
    head = head.astype(bf16).reshape(4, part, half)
    head = lax.all_to_all(head, ("xl", "xh"), split_axis=0, concat_axis=0, tiled=True)
    head = jnp.sum(head.astype(f32), axis=0)

    grad_own = lax.dynamic_slice(grad_proj, (y * own, 0), (own, width))
    weights_text, weights_text_other = (
        lax.dynamic_slice(w, (0, y * own), (rows, own)) for w in (weights_same, weights_other)
    )
    grad_own, weights_text, weights_text_other, image_unit, sent = lax.optimization_barrier(
        (grad_own, weights_text, weights_text_other, image_unit, sent)
    )
    grad_normed = dot(grad_own, weight, 1, 1)
    scaled = grad_normed * final_norm_gain
    first_mean = jnp.mean(scaled, axis=1, keepdims=True)
    second_mean = jnp.mean(scaled * xhat, axis=1, keepdims=True)
    grad_features = inverse_deviation * (scaled - first_mean - xhat * second_mean)
    vectors = jnp.stack([jnp.sum(grad_normed * xhat, axis=0), jnp.sum(grad_normed, axis=0)], 0)
    vectors = jnp.sum(spread_to(vectors, ("y", "xl", "xh", "core")), axis=0)

    lanes = 128
    lines = part // 4

    def payload(head_rows, vector):
        lead = vector.shape[:-1]
        high, low = (t.reshape(lead + (-1, lanes)) for t in split16(vector))
        rest = jnp.zeros(lead + (lines - 2 * high.shape[-2], lanes), bf16)
        side = jnp.concatenate([high, low, rest], -2)
        return jnp.concatenate([head_rows.astype(bf16), side], -1)

    def unpack(received):
        side = received[..., half:]
        count = 2 * width // 4 // lanes
        vector = side[..., :count, :] + side[..., count : 2 * count, :]
        return received[..., :half], vector.reshape(vector.shape[:-2] + (-1,))

    sent = payload(head.reshape(4, lines, half), vectors.reshape(4, 2 * width // 4))
    received = lax.all_to_all(sent, "zl", split_axis=0, concat_axis=0, tiled=True).astype(f32)
    received = spread_to(payload(*unpack(jnp.sum(received, axis=0))), "zh").astype(f32)
    sent = payload(*unpack(jnp.sum(received, axis=0)))
    received = spread_to(sent, ("zl", "xh")).reshape(4, 2, lines, half + lanes)
    vector_all = unpack(received[:, 0].astype(f32))[1].reshape(2, width) / 64.0
    head_all = received[..., :half].transpose(1, 0, 2, 3).reshape(2 * part, half)
    head_all = halves(core, head_all, shift(head_all, "core", 1), 1).astype(f32) / 64.0

    grad_unit_text = dot(weights_text, image_unit, 0, 0) + shift(
        dot(weights_text_other, image_unit, 0, 0), "core", 1
    )
    grad_unit_text = scale * grad_unit_text
    text_dot = jnp.sum(text_values * grad_unit_text, axis=1, keepdims=True)
    grad_text = inv_text * grad_unit_text - inv_text * inv_text * inv_text * text_dot * text_values

    return (
        swap(grad_features.astype(bf16)).astype(f32),
        swap(grad_text.astype(bf16)).astype(f32),
        vector_all[0],
        vector_all[1],
        head_all,
    )


def solution(mesh):
    fine = Mesh(mesh.devices.reshape(SIZES), AXES)
    placed = (P(ROWS, None), P(), P(), P(("y", "xl"), None), P(ROWS, None), P(), P())
    return jax.shard_map(
        local,
        mesh=fine,
        in_specs=placed,
        out_specs=(P(ROWS, None), P(ROWS, None), P(), P(), P(("y", "xl"), None)),
        check_vma=False,
    )
```

```python
import jax
import jax.numpy as jnp
from jax import lax
from jax.sharding import Mesh, PartitionSpec as P

epsilon = 1e-06
loss_scale = 64.0
AXES = ("y", "xl", "zh", "zl", "xh", "core")
SIZES = (4, 2, 4, 4, 2, 2)
ROWS = ("zh", "zl", "xh", "core", "y", "xl")
bf16 = jnp.bfloat16
f32 = jnp.float32


def shift(value, axis, steps):
    count = lax.axis_size(axis)
    return lax.ppermute(value, axis, [(i, (i + steps) % count) for i in range(count)])


def shift_x(value, steps):
    def index(place):
        place = place % 4
        return (place % 2) * 2 + place // 2

    return lax.ppermute(value, ("xl", "xh"), [(index(i), index(i + steps)) for i in range(4)])


def swap(value):
    return lax.ppermute(value, ("xl", "core"), [(0, 0), (1, 2), (2, 1), (3, 3)])


def halves(flag, first, second, axis):
    return jnp.where(
        flag == 0,
        jnp.concatenate([first, second], axis),
        jnp.concatenate([second, first], axis),
    )


def dot(a, b, da, db):
    return lax.dot_general(a, b, (((da,), (db,)), ((), ())), preferred_element_type=f32)


def split16(value):
    high = value.astype(bf16)
    return high, (value - high.astype(f32)).astype(bf16)


def spread_to(value, axes):
    count = lax.axis_size(axes)
    many = jnp.broadcast_to(value[None], (count,) + value.shape)
    return lax.all_to_all(many, axes, split_axis=0, concat_axis=0, tiled=True)


def after(value, *others):
    return lax.optimization_barrier((value,) + others)[0]


def place_y(value, y):
    rows, width = value.shape
    whole = jnp.zeros((4 * rows, width), bf16)
    moved = [(0, value)] + [(-step, shift(value, "y", step)) for step in (1, -1, 2)]
    for step, block in moved:
        whole = lax.dynamic_update_slice(whole, block, ((y + step) % 4 * rows, 0))
    return whole


def gather_weight(blocks, xl, core, earlier):
    count, rows, half = blocks.shape
    other = [shift_x(blocks[:2], 1), shift_x(blocks[2:], -1)]
    own_half = jnp.zeros((count, 2, rows, half), bf16)
    own_half = lax.dynamic_update_slice(own_half, blocks[:, None], (0, xl, 0, 0))
    for start, block in zip((0, 2), other):
        own_half = lax.dynamic_update_slice(own_half, block[:, None], (start, 1 - xl, 0, 0))
    own_half = after(own_half.reshape(2 * count * rows, half), earlier)
    weight = jnp.zeros((2 * count * rows, 2 * half), bf16)
    weight = lax.dynamic_update_slice(weight, own_half, (0, core * half))
    return lax.dynamic_update_slice(weight, shift(own_half, "core", 1), (0, (1 - core) * half))


def local(
    image_features, final_norm_gain, final_norm_bias, head_weight, text_embed, log_scale, logit_bias
):
    y, xl, xh, core = (lax.axis_index(a) for a in ("y", "xl", "xh", "core"))
    scale = jnp.exp(log_scale[0])
    offset = logit_bias[0]
    own, width = image_features.shape
    half = width // 2
    block = width // 4

    text_rows = swap(text_embed)
    feature_rows = swap(image_features)
    weight_part = lax.dynamic_slice(head_weight, (0, core * half), (head_weight.shape[0], half))
    weight_blocks = spread_to(weight_part, "y")

    text_values = text_rows.astype(f32)
    inv_text = lax.rsqrt(jnp.sum(text_values * text_values, axis=1, keepdims=True) + epsilon)
    text_unit = (text_values * inv_text).astype(bf16)

    values = feature_rows.astype(f32)
    centre = jnp.mean(values, axis=1, keepdims=True)
    centered = values - centre
    spread = jnp.mean(centered * centered, axis=1, keepdims=True)
    inverse_deviation = lax.rsqrt(spread + epsilon)
    xhat = centered * inverse_deviation
    normed_own = (xhat * final_norm_gain + final_norm_bias).astype(bf16)

    weight_blocks, text_unit, normed_own = lax.optimization_barrier(
        (weight_blocks, text_unit, normed_own)
    )
    text_same = place_y(text_unit, y)
    weight = gather_weight(weight_blocks, xl, core, text_same)
    normed = place_y(normed_own, y)
    text_other = shift(text_same, "core", 1)
    rows = normed.shape[0]

    projected = dot(normed, weight, 1, 0)
    inv_proj = lax.rsqrt(jnp.sum(projected * projected, axis=1, keepdims=True) + epsilon)
    image_unit = (projected * inv_proj).astype(bf16)

    def weights_of(text_rows, diagonal):
        logits = scale * dot(image_unit, text_rows, 1, 1) + offset
        return (loss_scale * (jax.nn.sigmoid(logits) - diagonal)).astype(bf16)

    weights_same = weights_of(text_same, jnp.eye(rows, dtype=f32))
    weights_other = weights_of(text_other, 0.0)
    grad_image = scale * (dot(weights_same, text_same, 1, 0) + dot(weights_other, text_other, 1, 0))
    proj_dot = jnp.sum(projected * grad_image, axis=1, keepdims=True)
    grad_proj = (
        inv_proj * grad_image - inv_proj * inv_proj * inv_proj * proj_dot * projected
    ).astype(bf16)

    normed_block = lax.dynamic_slice(normed, (0, y * block), (rows, block))
    theirs = lax.dynamic_slice(grad_proj, (0, (1 - core) * half), (rows, half))
    sent = dot(normed_block, theirs, 0, 0).astype(bf16)
    grad_proj, sent = lax.optimization_barrier((grad_proj, sent))
    mine = lax.dynamic_slice(grad_proj, (0, core * half), (rows, half))
    head = dot(normed_block, mine, 0, 0) + shift(sent, "core", 1).astype(f32)
    part = block // 4
    head = head.astype(bf16).reshape(4, part, half)
    head = lax.all_to_all(head, ("xl", "xh"), split_axis=0, concat_axis=0, tiled=True)
    head = jnp.sum(head.astype(f32), axis=0)

    grad_own = lax.dynamic_slice(grad_proj, (y * own, 0), (own, width))
    grad_normed = dot(grad_own, weight, 1, 1)
    vectors = jnp.stack([jnp.sum(grad_normed * xhat, axis=0), jnp.sum(grad_normed, axis=0)], 0)
    vectors = jnp.sum(spread_to(vectors, ("y", "xl")), axis=0)

    held = after((weights_same, weights_other, image_unit), head)
    text_part, text_theirs = (
        dot(lax.dynamic_slice(w, (0, y * own), (rows, own)), held[2], 0, 0) for w in held[:2]
    )
    grad_unit_text = text_part + shift(text_theirs, "core", 1)

    lanes = 128
    lines = part // 4
    count = 2 * width // 4 // lanes

    def payload(head_rows, vector):
        lead = vector.shape[:-1]
        high, low = (t.reshape(lead + (-1, lanes)) for t in split16(vector))
        rest = jnp.zeros(lead + (lines - 2 * count, lanes), bf16)
        side = jnp.concatenate([high, low, rest], -2)
        return jnp.concatenate([head_rows.astype(bf16), side], -1)

    def unpack(received):
        side = received[..., half:]
        vector = side[..., :count, :] + side[..., count : 2 * count, :]
        return received[..., :half], vector.reshape(vector.shape[:-2] + (-1,))

    sent = payload(head.reshape(4, lines, half), vectors.reshape(4, 2 * width // 4))
    received = lax.all_to_all(sent, "zl", split_axis=0, concat_axis=0, tiled=True).astype(f32)
    sent = payload(*unpack(jnp.sum(received, axis=0)))

    grad_unit_text, grad_normed = after((grad_unit_text, grad_normed), sent)
    grad_unit_text = scale * grad_unit_text
    text_dot = jnp.sum(text_values * grad_unit_text, axis=1, keepdims=True)
    grad_text = inv_text * grad_unit_text - inv_text * inv_text * inv_text * text_dot * text_values
    scaled = grad_normed * final_norm_gain
    first_mean = jnp.mean(scaled, axis=1, keepdims=True)
    second_mean = jnp.mean(scaled * xhat, axis=1, keepdims=True)
    grad_features = inverse_deviation * (scaled - first_mean - xhat * second_mean)
    returned = swap(jnp.stack([grad_features, grad_text], 0).astype(bf16))

    received = spread_to(sent, "zh").astype(f32)
    sent = payload(*unpack(jnp.sum(received, axis=0)))
    received = spread_to(sent, ("zl", "xh")).reshape(4, 2, lines, half + lanes)
    head_all = received[..., :half].transpose(1, 0, 2, 3).reshape(2 * part, half)
    vector_all = jnp.sum(unpack(received.astype(f32))[1], axis=1).reshape(-1, lanes)
    other_head, other_vector = shift(head_all, "core", 1), shift(vector_all, "core", 1)
    head_all = halves(core, head_all, other_head, 1).astype(f32) / 64.0
    vector_all = (vector_all + other_vector).reshape(2, width) / 64.0

    return (
        returned[0].astype(f32),
        returned[1].astype(f32),
        vector_all[0],
        vector_all[1],
        head_all,
    )


def solution(mesh):
    fine = Mesh(mesh.devices.reshape(SIZES), AXES)
    placed = (P(ROWS, None), P(), P(), P(("y", "xl"), None), P(ROWS, None), P(), P())
    return jax.shard_map(
        local,
        mesh=fine,
        in_specs=placed,
        out_specs=(P(ROWS, None), P(ROWS, None), P(), P(), P(("y", "xl"), None)),
        check_vma=False,
    )
```

```python
import jax
import jax.numpy as jnp
from jax import lax
from jax.sharding import Mesh, PartitionSpec as P

epsilon = 1e-06
loss_scale = 64.0
AXES = ("y", "xl", "zh", "zl", "xh", "core")
SIZES = (4, 2, 4, 4, 2, 2)
ROWS = ("zh", "zl", "xh", "core", "y", "xl")
bf16 = jnp.bfloat16
f32 = jnp.float32


def shift(value, axis, steps):
    count = lax.axis_size(axis)
    return lax.ppermute(value, axis, [(i, (i + steps) % count) for i in range(count)])


def shift_x(value, steps):
    def index(place):
        place = place % 4
        return (place % 2) * 2 + place // 2

    return lax.ppermute(value, ("xl", "xh"), [(index(i), index(i + steps)) for i in range(4)])


def swap(value):
    return lax.ppermute(value, ("xl", "core"), [(0, 0), (1, 2), (2, 1), (3, 3)])


def halves(flag, first, second, axis):
    return jnp.where(
        flag == 0,
        jnp.concatenate([first, second], axis),
        jnp.concatenate([second, first], axis),
    )


def dot(a, b, da, db):
    return lax.dot_general(a, b, (((da,), (db,)), ((), ())), preferred_element_type=f32)


def split16(value):
    high = value.astype(bf16)
    return high, (value - high.astype(f32)).astype(bf16)


def spread_to(value, axes):
    count = lax.axis_size(axes)
    many = jnp.broadcast_to(value[None], (count,) + value.shape)
    return lax.all_to_all(many, axes, split_axis=0, concat_axis=0, tiled=True)


def after(value, *others):
    return lax.optimization_barrier((value,) + others)[0]


def place_y(value, y):
    rows, width = value.shape
    half = rows // 2
    below, above = shift(value, "y", 1), shift(value, "y", -1)
    far = [shift(above[:half], "y", -1), shift(below[half:], "y", 1)]
    whole = jnp.zeros((4 * rows, width), bf16)
    for step, start, block in ((0, 0, value), (3, 0, below), (1, 0, above), (2, 0, far[0]), (2, half, far[1])):
        whole = lax.dynamic_update_slice(whole, block, ((y + step) % 4 * rows + start, 0))
    return whole, below, above


def gather_weight(blocks, xl, core, earlier):
    count, rows, half = blocks.shape
    other = [shift_x(blocks[:2], 1), shift_x(blocks[2:], -1)]
    own_half = jnp.zeros((count, 2, rows, half), bf16)
    own_half = lax.dynamic_update_slice(own_half, blocks[:, None], (0, xl, 0, 0))
    for start, block in zip((0, 2), other):
        own_half = lax.dynamic_update_slice(own_half, block[:, None], (start, 1 - xl, 0, 0))
    own_half = after(own_half.reshape(2 * count * rows, half), *earlier)
    weight = jnp.zeros((2 * count * rows, 2 * half), bf16)
    weight = lax.dynamic_update_slice(weight, own_half, (0, core * half))
    return lax.dynamic_update_slice(weight, shift(own_half, "core", 1), (0, (1 - core) * half))


def local(
    image_features, final_norm_gain, final_norm_bias, head_weight, text_embed, log_scale, logit_bias
):
    y, xl, xh, core = (lax.axis_index(a) for a in ("y", "xl", "xh", "core"))
    scale = jnp.exp(log_scale[0])
    offset = logit_bias[0]
    own, width = image_features.shape
    half = width // 2
    block = width // 4

    text_rows = swap(text_embed)
    feature_rows = swap(image_features)
    weight_part = lax.dynamic_slice(head_weight, (0, core * half), (head_weight.shape[0], half))
    weight_blocks = spread_to(weight_part, "y")

    text_values = text_rows.astype(f32)
    inv_text = lax.rsqrt(jnp.sum(text_values * text_values, axis=1, keepdims=True) + epsilon)
    text_unit = (text_values * inv_text).astype(bf16)

    values = feature_rows.astype(f32)
    centre = jnp.mean(values, axis=1, keepdims=True)
    centered = values - centre
    spread = jnp.mean(centered * centered, axis=1, keepdims=True)
    inverse_deviation = lax.rsqrt(spread + epsilon)
    xhat = centered * inverse_deviation
    normed_own = (xhat * final_norm_gain + final_norm_bias).astype(bf16)

    text_same = place_y(text_unit, y)[0]
    normed, *neighbours = place_y(normed_own, y)
    weight_blocks = after(weight_blocks, text_unit, normed_own)
    weight = gather_weight(weight_blocks, xl, core, [text_same] + neighbours)
    text_other = shift(text_same, "core", 1)
    rows = normed.shape[0]

    projected = dot(normed, weight, 1, 0)
    inv_proj = lax.rsqrt(jnp.sum(projected * projected, axis=1, keepdims=True) + epsilon)
    image_unit = (projected * inv_proj).astype(bf16)

    def weights_of(text_rows, diagonal):
        logits = scale * dot(image_unit, text_rows, 1, 1) + offset
        return (loss_scale * (jax.nn.sigmoid(logits) - diagonal)).astype(bf16)

    weights_same = weights_of(text_same, jnp.eye(rows, dtype=f32))
    weights_other = weights_of(text_other, 0.0)
    grad_image = scale * (dot(weights_same, text_same, 1, 0) + dot(weights_other, text_other, 1, 0))
    proj_dot = jnp.sum(projected * grad_image, axis=1, keepdims=True)
    grad_proj = (
        inv_proj * grad_image - inv_proj * inv_proj * inv_proj * proj_dot * projected
    ).astype(bf16)

    normed_block = lax.dynamic_slice(normed, (0, y * block), (rows, block))
    theirs = lax.dynamic_slice(grad_proj, (0, (1 - core) * half), (rows, half))
    sent = dot(normed_block, theirs, 0, 0).astype(bf16)
    grad_proj, sent = lax.optimization_barrier((grad_proj, sent))
    mine = lax.dynamic_slice(grad_proj, (0, core * half), (rows, half))
    head = dot(normed_block, mine, 0, 0) + shift(sent, "core", 1).astype(f32)
    part = block // 4
    head = head.astype(bf16).reshape(4, part, half)
    head_sent = head
    head = lax.all_to_all(head, ("xl", "xh"), split_axis=0, concat_axis=0, tiled=True)
    head = jnp.sum(head.astype(f32), axis=0)

    grad_own = lax.dynamic_slice(grad_proj, (y * own, 0), (own, width))
    grad_normed = dot(grad_own, weight, 1, 1)
    vectors = jnp.stack([jnp.sum(grad_normed * xhat, axis=0), jnp.sum(grad_normed, axis=0)], 0)
    vectors = jnp.sum(spread_to(after(vectors, head_sent), ("y", "xl", "core")), axis=0)

    held = after((weights_same, weights_other, image_unit), head)
    text_part, text_theirs = (
        dot(lax.dynamic_slice(w, (0, y * own), (rows, own)), held[2], 0, 0) for w in held[:2]
    )
    grad_unit_text = text_part + shift(text_theirs, "core", 1)

    lanes = 128
    lines = part // 4
    count = 2 * width // 4 // lanes

    def payload(head_rows, vector):
        lead = vector.shape[:-1]
        high, low = (t.reshape(lead + (-1, lanes)) for t in split16(vector))
        rest = jnp.zeros(lead + (lines - 2 * count, lanes), bf16)
        side = jnp.concatenate([high, low, rest], -2)
        return jnp.concatenate([head_rows.astype(bf16), side], -1)

    def unpack(received):
        side = received[..., half:]
        vector = side[..., :count, :] + side[..., count : 2 * count, :]
        return received[..., :half], vector.reshape(vector.shape[:-2] + (-1,))

    sent = payload(head.reshape(4, lines, half), vectors.reshape(4, 2 * width // 4))
    received = lax.all_to_all(sent, "zl", split_axis=0, concat_axis=0, tiled=True).astype(f32)
    sent = payload(*unpack(jnp.sum(received, axis=0)))

    grad_unit_text, grad_normed = after((grad_unit_text, grad_normed), sent)
    grad_unit_text = scale * grad_unit_text
    text_dot = jnp.sum(text_values * grad_unit_text, axis=1, keepdims=True)
    grad_text = inv_text * grad_unit_text - inv_text * inv_text * inv_text * text_dot * text_values
    scaled = grad_normed * final_norm_gain
    first_mean = jnp.mean(scaled, axis=1, keepdims=True)
    second_mean = jnp.mean(scaled * xhat, axis=1, keepdims=True)
    grad_features = inverse_deviation * (scaled - first_mean - xhat * second_mean)
    returned = swap(jnp.stack([grad_features, grad_text], 0).astype(bf16))

    received = spread_to(sent, "zh").astype(f32)
    sent = payload(*unpack(jnp.sum(received, axis=0)))
    received = spread_to(sent, ("zl", "xh")).reshape(4, 2, lines, half + lanes)
    head_all = received[..., :half].transpose(1, 0, 2, 3).reshape(2 * part, half)
    vector_all = jnp.sum(unpack(received.astype(f32))[1], axis=1).reshape(2, width) / 64.0
    head_all = halves(core, head_all, shift(head_all, "core", 1), 1).astype(f32) / 64.0

    return (
        returned[0].astype(f32),
        returned[1].astype(f32),
        vector_all[0],
        vector_all[1],
        head_all,
    )


def solution(mesh):
    fine = Mesh(mesh.devices.reshape(SIZES), AXES)
    placed = (P(ROWS, None), P(), P(), P(("y", "xl"), None), P(ROWS, None), P(), P())
    return jax.shard_map(
        local,
        mesh=fine,
        in_specs=placed,
        out_specs=(P(ROWS, None), P(ROWS, None), P(), P(), P(("y", "xl"), None)),
        check_vma=False,
    )
```

```python
import jax
import jax.numpy as jnp
from jax import lax
from jax.sharding import Mesh, PartitionSpec as P

epsilon = 1e-06
loss_scale = 64.0
AXES = ("y", "xl", "zh", "zl", "xh", "core")
SIZES = (4, 2, 4, 4, 2, 2)
ROWS = ("zh", "zl", "xh", "core", "y", "xl")
bf16 = jnp.bfloat16
f32 = jnp.float32


def shift(value, axis, steps):
    count = lax.axis_size(axis)
    return lax.ppermute(value, axis, [(i, (i + steps) % count) for i in range(count)])


def shift_x(value, steps):
    def index(place):
        place = place % 4
        return (place % 2) * 2 + place // 2

    return lax.ppermute(value, ("xl", "xh"), [(index(i), index(i + steps)) for i in range(4)])


def swap(value):
    return lax.ppermute(value, ("xl", "core"), [(0, 0), (1, 2), (2, 1), (3, 3)])


def halves(flag, first, second, axis):
    return jnp.where(
        flag == 0,
        jnp.concatenate([first, second], axis),
        jnp.concatenate([second, first], axis),
    )


def dot(a, b, da, db):
    return lax.dot_general(a, b, (((da,), (db,)), ((), ())), preferred_element_type=f32)


def split16(value):
    high = value.astype(bf16)
    return high, (value - high.astype(f32)).astype(bf16)


def spread_to(value, axes):
    count = lax.axis_size(axes)
    many = jnp.broadcast_to(value[None], (count,) + value.shape)
    return lax.all_to_all(many, axes, split_axis=0, concat_axis=0, tiled=True)


def after(value, *others):
    return lax.optimization_barrier((value,) + others)[0]


def gather_weight(blocks, xl, core):
    count, rows, half = blocks.shape
    other = [shift_x(blocks[:2], 1), shift_x(blocks[2:], -1)]
    own_half = jnp.zeros((count, 2, rows, half), bf16)
    own_half = lax.dynamic_update_slice(own_half, blocks[:, None], (0, xl, 0, 0))
    for start, block in zip((0, 2), other):
        own_half = lax.dynamic_update_slice(own_half, block[:, None], (start, 1 - xl, 0, 0))
    own_half = own_half.reshape(2 * count * rows, half)
    weight = jnp.zeros((2 * count * rows, 2 * half), bf16)
    weight = lax.dynamic_update_slice(weight, own_half, (0, core * half))
    weight = lax.dynamic_update_slice(weight, shift(own_half, "core", 1), (0, (1 - core) * half))
    return weight, own_half


def place_y(value, y, early, late):
    arrays, rows, width = value.shape
    moved = [(3, shift(value, "y", 1)), (1, shift(value, "y", -1)), (2, shift(value, "y", 2))]
    moved[0] = (3, after(moved[0][1], early))
    moved[1] = (1, after(moved[1][1], early))
    moved[2] = (2, after(moved[2][1], late))
    results = []
    for index in range(arrays):
        whole = jnp.zeros((4 * rows, width), bf16)
        for step, blocks in [(0, value)] + moved:
            whole = lax.dynamic_update_slice(whole, blocks[index], ((y + step) % 4 * rows, 0))
        results.append(whole)
    return results


def local(
    image_features, final_norm_gain, final_norm_bias, head_weight, text_embed, log_scale, logit_bias
):
    y, xl, xh, core = (lax.axis_index(a) for a in ("y", "xl", "xh", "core"))
    scale = jnp.exp(log_scale[0])
    offset = logit_bias[0]
    own, width = image_features.shape
    half = width // 2
    block = width // 4

    text_rows, feature_rows = swap(jnp.stack([text_embed, image_features], 0))
    weight_part = lax.dynamic_slice(head_weight, (0, core * half), (head_weight.shape[0], half))
    weight_blocks = spread_to(weight_part, "y")

    text_values = text_rows.astype(f32)
    inv_text = lax.rsqrt(jnp.sum(text_values * text_values, axis=1, keepdims=True) + epsilon)
    text_unit = (text_values * inv_text).astype(bf16)

    values = feature_rows.astype(f32)
    centre = jnp.mean(values, axis=1, keepdims=True)
    centered = values - centre
    spread = jnp.mean(centered * centered, axis=1, keepdims=True)
    inverse_deviation = lax.rsqrt(spread + epsilon)
    xhat = centered * inverse_deviation
    normed_own = (xhat * final_norm_gain + final_norm_bias).astype(bf16)

    weight, own_half = gather_weight(after(weight_blocks, text_unit, normed_own), xl, core)
    text_same, normed = place_y(jnp.stack([text_unit, normed_own], 0), y, own_half, weight)
    text_other = shift(text_same, "core", 1)
    rows = normed.shape[0]

    projected = dot(normed, weight, 1, 0)
    inv_proj = lax.rsqrt(jnp.sum(projected * projected, axis=1, keepdims=True) + epsilon)
    image_unit = (projected * inv_proj).astype(bf16)

    def weights_of(text_rows, diagonal):
        logits = scale * dot(image_unit, text_rows, 1, 1) + offset
        return (loss_scale * (jax.nn.sigmoid(logits) - diagonal)).astype(bf16)

    weights_same = weights_of(text_same, jnp.eye(rows, dtype=f32))
    weights_other = weights_of(text_other, 0.0)
    grad_image = scale * (dot(weights_same, text_same, 1, 0) + dot(weights_other, text_other, 1, 0))
    proj_dot = jnp.sum(projected * grad_image, axis=1, keepdims=True)
    grad_proj = (
        inv_proj * grad_image - inv_proj * inv_proj * inv_proj * proj_dot * projected
    ).astype(bf16)

    normed_block = lax.dynamic_slice(normed, (0, y * block), (rows, block))
    theirs = lax.dynamic_slice(grad_proj, (0, (1 - core) * half), (rows, half))
    sent = dot(normed_block, theirs, 0, 0).astype(bf16)
    grad_proj, sent = lax.optimization_barrier((grad_proj, sent))
    mine = lax.dynamic_slice(grad_proj, (0, core * half), (rows, half))
    head = dot(normed_block, mine, 0, 0) + shift(sent, "core", 1).astype(f32)
    part = block // 4
    lanes = 128

    grad_own = lax.dynamic_slice(grad_proj, (y * own, 0), (own, width))
    grad_normed = dot(grad_own, weight, 1, 1)
    vectors = jnp.stack([jnp.sum(grad_normed * xhat, axis=0), jnp.sum(grad_normed, axis=0)], 0)

    def payload(head_rows, vector):
        lead, lines = head_rows.shape[:-2], head_rows.shape[-2]
        high, low = (t.reshape(lead + (-1, lanes)) for t in split16(vector))
        rest = jnp.zeros(lead + (lines - 2 * high.shape[-2], lanes), bf16)
        side = jnp.concatenate([high, low, rest], -2)
        return jnp.concatenate([head_rows.astype(bf16), side], -1)

    def unpack(received, count):
        side = received[..., half:]
        vector = side[..., :count, :] + side[..., count : 2 * count, :]
        return received[..., :half], vector

    halved = jnp.broadcast_to(vectors.reshape(1, 2, width), (2, 2, width)).reshape(4, width)
    sent = payload(head.reshape(4, part, half), halved)
    received = lax.all_to_all(sent, ("xl", "xh"), split_axis=0, concat_axis=0, tiled=True)
    head, vector = unpack(jnp.sum(received.astype(f32), axis=0), width // lanes)

    held = after((weights_same, weights_other, image_unit), head)
    text_part, text_theirs = (
        dot(lax.dynamic_slice(w, (0, y * own), (rows, own)), held[2], 0, 0) for w in held[:2]
    )
    grad_unit_text = text_part + shift(text_theirs, "core", 1)

    lines = part // 4
    count = width // 4 // lanes
    sent = payload(head.reshape(4, lines, half), vector.reshape(4, width // 4))
    received = lax.all_to_all(sent, "zl", split_axis=0, concat_axis=0, tiled=True).astype(f32)
    sent = payload(*unpack(jnp.sum(received, axis=0), count))

    grad_unit_text, grad_normed = after((grad_unit_text, grad_normed), sent)
    grad_unit_text = scale * grad_unit_text
    text_dot = jnp.sum(text_values * grad_unit_text, axis=1, keepdims=True)
    grad_text = inv_text * grad_unit_text - inv_text * inv_text * inv_text * text_dot * text_values
    scaled = grad_normed * final_norm_gain
    first_mean = jnp.mean(scaled, axis=1, keepdims=True)
    second_mean = jnp.mean(scaled * xhat, axis=1, keepdims=True)
    grad_features = inverse_deviation * (scaled - first_mean - xhat * second_mean)
    returned = swap(jnp.stack([grad_features, grad_text], 0).astype(bf16))

    received = spread_to(sent, "zh").astype(f32)
    sent = payload(*unpack(jnp.sum(received, axis=0), count))
    received = spread_to(sent, ("zl", "xh")).reshape(4, 2, lines, half + lanes)
    head_all = received[..., :half].transpose(1, 0, 2, 3).reshape(2 * part, half)
    vectors = unpack(received.astype(f32), count)[1].transpose(1, 0, 2, 3).reshape(2, width)
    vectors = jnp.sum(spread_to(vectors, ("y", "core")), axis=0) / 64.0
    head_all = halves(core, head_all, shift(head_all, "core", 1), 1).astype(f32) / 64.0

    return (
        returned[0].astype(f32),
        returned[1].astype(f32),
        vectors[0],
        vectors[1],
        head_all,
    )


def solution(mesh):
    fine = Mesh(mesh.devices.reshape(SIZES), AXES)
    placed = (P(ROWS, None), P(), P(), P(("y", "xl"), None), P(ROWS, None), P(), P())
    return jax.shard_map(
        local,
        mesh=fine,
        in_specs=placed,
        out_specs=(P(ROWS, None), P(ROWS, None), P(), P(), P(("y", "xl"), None)),
        check_vma=False,
    )
```

```python
import jax
import jax.numpy as jnp
from jax import lax
from jax.sharding import Mesh, PartitionSpec as P

epsilon = 1e-06
loss_scale = 64.0
AXES = ("y", "xl", "zh", "zl", "xh", "core")
SIZES = (4, 2, 4, 4, 2, 2)
ROWS = ("zh", "zl", "xh", "core", "y", "xl")
bf16 = jnp.bfloat16
f32 = jnp.float32


def shift(value, axis, steps):
    count = lax.axis_size(axis)
    return lax.ppermute(value, axis, [(i, (i + steps) % count) for i in range(count)])


def shift_x(value, steps):
    def index(place):
        place = place % 4
        return (place % 2) * 2 + place // 2

    return lax.ppermute(value, ("xl", "xh"), [(index(i), index(i + steps)) for i in range(4)])


def swap(value):
    return lax.ppermute(value, ("xl", "core"), [(0, 0), (1, 2), (2, 1), (3, 3)])


def halves(flag, first, second, axis):
    return jnp.where(
        flag == 0,
        jnp.concatenate([first, second], axis),
        jnp.concatenate([second, first], axis),
    )


def dot(a, b, da, db):
    return lax.dot_general(a, b, (((da,), (db,)), ((), ())), preferred_element_type=f32)


def split16(value):
    high = value.astype(bf16)
    return high, (value - high.astype(f32)).astype(bf16)


def spread_to(value, axes):
    count = lax.axis_size(axes)
    many = jnp.broadcast_to(value[None], (count,) + value.shape)
    return lax.all_to_all(many, axes, split_axis=0, concat_axis=0, tiled=True)


def after(value, *others):
    return lax.optimization_barrier((value,) + others)[0]


def gather_weight(blocks, xl, core, earlier):
    count, rows, half = blocks.shape
    other = [shift_x(blocks[:2], 1), shift_x(blocks[2:], -1)]
    own_half = jnp.zeros((count, 2, rows, half), bf16)
    own_half = lax.dynamic_update_slice(own_half, blocks[:, None], (0, xl, 0, 0))
    for start, block in zip((0, 2), other):
        own_half = lax.dynamic_update_slice(own_half, block[:, None], (start, 1 - xl, 0, 0))
    own_half = after(own_half.reshape(2 * count * rows, half), *earlier)
    weight = jnp.zeros((2 * count * rows, 2 * half), bf16)
    weight = lax.dynamic_update_slice(weight, own_half, (0, core * half))
    weight = lax.dynamic_update_slice(weight, shift(own_half, "core", 1), (0, (1 - core) * half))
    return weight


def placed(blocks):
    rows, width = blocks[0].shape
    whole = lax.optimization_barrier(jnp.zeros((len(blocks) * rows, width), blocks[0].dtype))
    for index, block in enumerate(blocks):
        whole = lax.dynamic_update_slice(whole, block, (index * rows, 0))
    return whole


def standardize(block):
    values = block.astype(f32)
    centre = jnp.mean(values, axis=1, keepdims=True)
    centered = values - centre
    spread = jnp.mean(centered * centered, axis=1, keepdims=True)
    return centre, lax.rsqrt(spread + epsilon)


def local(
    image_features, final_norm_gain, final_norm_bias, head_weight, text_embed, log_scale, logit_bias
):
    y, xl, xh, core = (lax.axis_index(a) for a in ("y", "xl", "xh", "core"))
    scale = jnp.exp(log_scale[0])
    offset = logit_bias[0]
    own, width = image_features.shape
    half = width // 2
    block = width // 4

    text_rows, feature_rows = swap(jnp.stack([text_embed, image_features], 0))
    weight_part = lax.dynamic_slice(head_weight, (0, core * half), (head_weight.shape[0], half))
    weight_blocks = spread_to(weight_part, "y")

    text_values = text_rows.astype(f32)
    inv_text = lax.rsqrt(jnp.sum(text_values * text_values, axis=1, keepdims=True) + epsilon)
    text_unit = (text_values * inv_text).astype(bf16)

    pair = jnp.stack([text_unit, feature_rows], 0)
    below, above = shift(pair, "y", 1), shift(pair, "y", -1)
    weight = gather_weight(weight_blocks, xl, core, [below, above])
    text_far, feature_far = shift(above[0], "y", -1), shift(below[1], "y", 1)
    text_same = placed([text_unit, below[0], above[0], text_far])
    raw = [feature_rows, below[1], above[1], feature_far]
    stats = [standardize(block) for block in raw]
    normed = placed(
        [
            ((block.astype(f32) - centre) * inverse * final_norm_gain + final_norm_bias).astype(bf16)
            for block, (centre, inverse) in zip(raw, stats)
        ]
    )
    text_other = shift(text_same, "core", 1)
    rows = normed.shape[0]

    projected = dot(normed, weight, 1, 0)
    inv_proj = lax.rsqrt(jnp.sum(projected * projected, axis=1, keepdims=True) + epsilon)
    image_unit = (projected * inv_proj).astype(bf16)

    def weights_of(text_rows, diagonal):
        logits = scale * dot(image_unit, text_rows, 1, 1) + offset
        return (loss_scale * (jax.nn.sigmoid(logits) - diagonal)).astype(bf16)

    weights_same = weights_of(text_same, jnp.eye(rows, dtype=f32))
    weights_other = weights_of(text_other, 0.0)
    grad_image = scale * (dot(weights_same, text_same, 1, 0) + dot(weights_other, text_other, 1, 0))
    proj_dot = jnp.sum(projected * grad_image, axis=1, keepdims=True)
    grad_proj = (
        inv_proj * grad_image - inv_proj * inv_proj * inv_proj * proj_dot * projected
    ).astype(bf16)

    normed_block = lax.dynamic_slice(normed, (0, y * block), (rows, block))
    theirs = lax.dynamic_slice(grad_proj, (0, (1 - core) * half), (rows, half))
    sent = dot(normed_block, theirs, 0, 0).astype(bf16)
    grad_proj, sent = lax.optimization_barrier((grad_proj, sent))
    mine = lax.dynamic_slice(grad_proj, (0, core * half), (rows, half))
    head = dot(normed_block, mine, 0, 0) + shift(sent, "core", 1).astype(f32)
    part = block // 4
    lanes = 128

    grad_normed = dot(grad_proj, weight, 1, 1)
    centre = jnp.concatenate([part[0] for part in stats], 0)
    inverse_deviation = jnp.concatenate([part[1] for part in stats], 0)
    xhat = (placed(raw).astype(f32) - centre) * inverse_deviation
    vectors = jnp.stack([jnp.sum(grad_normed * xhat, axis=0), jnp.sum(grad_normed, axis=0)], 0)
    xhat, grad_normed, inverse_deviation = xhat[:own], grad_normed[:own], inverse_deviation[:own]

    def payload(head_rows, vector):
        lead, lines = head_rows.shape[:-2], head_rows.shape[-2]
        high, low = (t.reshape(lead + (-1, lanes)) for t in split16(vector))
        rest = jnp.zeros(lead + (lines - 2 * high.shape[-2], lanes), bf16)
        side = jnp.concatenate([high, low, rest], -2)
        return jnp.concatenate([head_rows.astype(bf16), side], -1)

    def unpack(received, count):
        side = received[..., half:]
        vector = side[..., :count, :] + side[..., count : 2 * count, :]
        return received[..., :half], vector

    halved = jnp.broadcast_to(vectors.reshape(1, 2, width), (2, 2, width)).reshape(4, width)
    sent = payload(head.reshape(4, part, half), halved)
    received = lax.all_to_all(sent, ("xl", "xh"), split_axis=0, concat_axis=0, tiled=True)
    head, vector = unpack(jnp.sum(received.astype(f32), axis=0), width // lanes)

    held = after((weights_same, weights_other, image_unit), head)
    text_part, text_theirs = (
        dot(w[:, :own], held[2], 0, 0) for w in held[:2]
    )
    grad_unit_text = text_part + shift(text_theirs, "core", 1)

    lines = part // 4
    count = width // 4 // lanes
    sent = payload(head.reshape(4, lines, half), vector.reshape(4, width // 4))
    received = lax.all_to_all(sent, "zl", split_axis=0, concat_axis=0, tiled=True).astype(f32)
    sent = payload(*unpack(jnp.sum(received, axis=0), count))

    grad_unit_text, grad_normed = after((grad_unit_text, grad_normed), sent)
    grad_unit_text = scale * grad_unit_text
    text_dot = jnp.sum(text_values * grad_unit_text, axis=1, keepdims=True)
    grad_text = inv_text * grad_unit_text - inv_text * inv_text * inv_text * text_dot * text_values
    scaled = grad_normed * final_norm_gain
    first_mean = jnp.mean(scaled, axis=1, keepdims=True)
    second_mean = jnp.mean(scaled * xhat, axis=1, keepdims=True)
    grad_features = inverse_deviation * (scaled - first_mean - xhat * second_mean)
    returned = swap(jnp.stack([grad_features, grad_text], 0).astype(bf16))

    received = spread_to(sent, "zh").astype(f32)
    sent = payload(*unpack(jnp.sum(received, axis=0), count))
    received = spread_to(sent, ("zl", "xh")).reshape(4, 2, lines, half + lanes)
    head_all = received[..., :half].transpose(1, 0, 2, 3).reshape(2 * part, half)
    vectors = unpack(received.astype(f32), count)[1].transpose(1, 0, 2, 3).reshape(2, width)
    sent = jnp.concatenate([head_all, *(t.reshape(-1, half) for t in split16(vectors))], 0)
    received = shift(sent, "core", 1)
    head_all = halves(core, head_all, received[: 2 * part], 1).astype(f32) / 64.0
    high, low = jnp.split(received[2 * part :].astype(f32), 2, 0)
    vectors = (vectors + (high + low).reshape(2, width)) / 64.0

    return (
        returned[0].astype(f32),
        returned[1].astype(f32),
        vectors[0],
        vectors[1],
        head_all,
    )


def solution(mesh):
    fine = Mesh(mesh.devices.reshape(SIZES), AXES)
    placed = (P(ROWS, None), P(), P(), P(("y", "xl"), None), P(ROWS, None), P(), P())
    return jax.shard_map(
        local,
        mesh=fine,
        in_specs=placed,
        out_specs=(P(ROWS, None), P(ROWS, None), P(), P(), P(("y", "xl"), None)),
        check_vma=False,
    )
```

```python
import jax
import jax.numpy as jnp
from jax import lax
from jax.sharding import Mesh, PartitionSpec as P

epsilon = 1e-06
loss_scale = 64.0
AXES = ("y", "xl", "zh", "zl", "xh", "core")
SIZES = (4, 2, 4, 4, 2, 2)
ROWS = ("zh", "zl", "xh", "core", "y", "xl")
bf16 = jnp.bfloat16
f32 = jnp.float32


def shift(value, axis, steps):
    count = lax.axis_size(axis)
    return lax.ppermute(value, axis, [(i, (i + steps) % count) for i in range(count)])


def shift_x(value, steps):
    def index(place):
        place = place % 4
        return (place % 2) * 2 + place // 2

    return lax.ppermute(value, ("xl", "xh"), [(index(i), index(i + steps)) for i in range(4)])


def swap(value):
    return lax.ppermute(value, ("xl", "core"), [(0, 0), (1, 2), (2, 1), (3, 3)])


def halves(flag, first, second, axis):
    return jnp.where(
        flag == 0,
        jnp.concatenate([first, second], axis),
        jnp.concatenate([second, first], axis),
    )


def dot(a, b, da, db):
    return lax.dot_general(a, b, (((da,), (db,)), ((), ())), preferred_element_type=f32)


def spread_to(value, axes):
    count = lax.axis_size(axes)
    many = jnp.broadcast_to(value[None], (count,) + value.shape)
    return lax.all_to_all(many, axes, split_axis=0, concat_axis=0, tiled=True)


def after(value, *others):
    return lax.optimization_barrier((value,) + others)[0]


def gather_weight(blocks, xl, core, earlier):
    count, rows, half = blocks.shape
    other = [shift_x(blocks[:2], 1), shift_x(blocks[2:], -1)]
    own_half = jnp.zeros((count, 2, rows, half), bf16)
    own_half = lax.dynamic_update_slice(own_half, blocks[:, None], (0, xl, 0, 0))
    for start, block in zip((0, 2), other):
        own_half = lax.dynamic_update_slice(own_half, block[:, None], (start, 1 - xl, 0, 0))
    own_half = after(own_half.reshape(2 * count * rows, half), *earlier)
    weight = jnp.zeros((2 * count * rows, 2 * half), bf16)
    weight = lax.dynamic_update_slice(weight, own_half, (0, core * half))
    weight = lax.dynamic_update_slice(weight, shift(own_half, "core", 1), (0, (1 - core) * half))
    return weight


def placed(blocks):
    rows, width = blocks[0].shape
    whole = lax.optimization_barrier(jnp.zeros((len(blocks) * rows, width), blocks[0].dtype))
    for index, block in enumerate(blocks):
        whole = lax.dynamic_update_slice(whole, block, (index * rows, 0))
    return whole


def standardize(block):
    values = block.astype(f32)
    centre = jnp.mean(values, axis=1, keepdims=True)
    centered = values - centre
    spread = jnp.mean(centered * centered, axis=1, keepdims=True)
    return centre, lax.rsqrt(spread + epsilon)


def local(
    image_features, final_norm_gain, final_norm_bias, head_weight, text_embed, log_scale, logit_bias
):
    y, xl, xh, core = (lax.axis_index(a) for a in ("y", "xl", "xh", "core"))
    scale = jnp.exp(log_scale[0])
    offset = logit_bias[0]
    own, width = image_features.shape
    half = width // 2
    block = width // 4

    text_rows, feature_rows = swap(jnp.stack([text_embed, image_features], 0))
    weight_part = lax.dynamic_slice(head_weight, (0, core * half), (head_weight.shape[0], half))
    weight_blocks = spread_to(weight_part, "y")

    text_values = text_rows.astype(f32)
    inv_text = lax.rsqrt(jnp.sum(text_values * text_values, axis=1, keepdims=True) + epsilon)
    text_unit = (text_values * inv_text).astype(bf16)

    pair = jnp.stack([text_unit, feature_rows], 0)
    below, above, far = shift(pair, "y", 1), shift(pair, "y", -1), shift(pair, "y", 2)
    weight = gather_weight(weight_blocks, xl, core, [below, above, far])
    text_same = placed([text_unit, below[0], above[0], far[0]])
    raw = [feature_rows, below[1], above[1], far[1]]
    stats = [standardize(block) for block in raw]
    normed = placed(
        [
            ((block.astype(f32) - centre) * inverse * final_norm_gain + final_norm_bias).astype(bf16)
            for block, (centre, inverse) in zip(raw, stats)
        ]
    )
    text_other = shift(text_same, "core", 1)
    rows = normed.shape[0]

    projected = dot(normed, weight, 1, 0)
    inv_proj = lax.rsqrt(jnp.sum(projected * projected, axis=1, keepdims=True) + epsilon)
    image_unit = (projected * inv_proj).astype(bf16)

    def weights_of(text_rows, diagonal):
        logits = scale * dot(image_unit, text_rows, 1, 1) + offset
        return (loss_scale * (jax.nn.sigmoid(logits) - diagonal)).astype(bf16)

    weights_same = weights_of(text_same, jnp.eye(rows, dtype=f32))
    weights_other = weights_of(text_other, 0.0)
    grad_image = scale * (dot(weights_same, text_same, 1, 0) + dot(weights_other, text_other, 1, 0))
    proj_dot = jnp.sum(projected * grad_image, axis=1, keepdims=True)
    grad_proj = (
        inv_proj * grad_image - inv_proj * inv_proj * inv_proj * proj_dot * projected
    ).astype(bf16)

    normed_block = lax.dynamic_slice(normed, (0, y * block), (rows, block))
    theirs = lax.dynamic_slice(grad_proj, (0, (1 - core) * half), (rows, half))
    sent = dot(normed_block, theirs, 0, 0).astype(bf16)
    grad_proj, sent = lax.optimization_barrier((grad_proj, sent))
    mine = lax.dynamic_slice(grad_proj, (0, core * half), (rows, half))
    head = dot(normed_block, mine, 0, 0) + shift(sent, "core", 1).astype(f32)
    part = block // 4
    lanes = 128

    grad_normed = dot(grad_proj, weight, 1, 1)
    centre = jnp.concatenate([part[0] for part in stats], 0)
    inverse_deviation = jnp.concatenate([part[1] for part in stats], 0)
    xhat = (placed(raw).astype(f32) - centre) * inverse_deviation
    vectors = jnp.stack([jnp.sum(grad_normed * xhat, axis=0), jnp.sum(grad_normed, axis=0)], 0)
    xhat, grad_normed, inverse_deviation = xhat[:own], grad_normed[:own], inverse_deviation[:own]

    lines = part // 4
    count = width // 4 // lanes
    side = vectors.astype(bf16).reshape(1, 2, 4, count, lanes)
    side = jnp.pad(side, ((0, 0), (0, 0), (0, 0), (0, lines - count), (0, 0)))
    side = jnp.broadcast_to(side, (2,) + side.shape[1:]).reshape(4, part, lanes)
    sent = jnp.concatenate([head.astype(bf16).reshape(4, part, half), side], -1)
    received = lax.all_to_all(sent, ("xl", "xh"), split_axis=0, concat_axis=0, tiled=True)
    head = jnp.sum(received.astype(f32), axis=0).astype(bf16)

    held = after((weights_same, weights_other, image_unit), head)
    text_part, text_theirs = (
        dot(w[:, :own], held[2], 0, 0) for w in held[:2]
    )
    grad_unit_text = text_part + shift(text_theirs, "core", 1)

    sent = head.reshape(4, lines, half + lanes)
    received = lax.all_to_all(sent, "zl", split_axis=0, concat_axis=0, tiled=True)
    sent = jnp.sum(received.astype(f32), axis=0).astype(bf16)

    grad_unit_text, grad_normed = after((grad_unit_text, grad_normed), sent)
    grad_unit_text = scale * grad_unit_text
    text_dot = jnp.sum(text_values * grad_unit_text, axis=1, keepdims=True)
    grad_text = inv_text * grad_unit_text - inv_text * inv_text * inv_text * text_dot * text_values
    scaled = grad_normed * final_norm_gain
    first_mean = jnp.mean(scaled, axis=1, keepdims=True)
    second_mean = jnp.mean(scaled * xhat, axis=1, keepdims=True)
    grad_features = inverse_deviation * (scaled - first_mean - xhat * second_mean)
    returned = swap(jnp.stack([grad_features, grad_text], 0).astype(bf16))

    received = spread_to(sent, "zh")
    sent = after(jnp.sum(received.astype(f32), axis=0).astype(bf16), returned)
    mine = spread_to(sent, ("zl", "xh"))
    theirs = shift(mine, "core", 1)

    def unpack(received):
        received = received.reshape(4, 2, lines, half + lanes).transpose(1, 0, 2, 3)
        vectors = received[..., :count, half:].astype(f32).reshape(2, width)
        return received[..., :half].reshape(2 * part, half), vectors

    (head_mine, vectors_mine), (head_theirs, vectors_theirs) = unpack(mine), unpack(theirs)
    head_all = halves(core, head_mine, head_theirs, 1).astype(f32) / 64.0
    vectors = (vectors_mine + vectors_theirs) / 64.0

    return (
        returned[0].astype(f32),
        returned[1].astype(f32),
        vectors[0],
        vectors[1],
        head_all,
    )


def solution(mesh):
    fine = Mesh(mesh.devices.reshape(SIZES), AXES)
    placed = (P(ROWS, None), P(), P(), P(("y", "xl"), None), P(ROWS, None), P(), P())
    return jax.shard_map(
        local,
        mesh=fine,
        in_specs=placed,
        out_specs=(P(ROWS, None), P(ROWS, None), P(), P(), P(("y", "xl"), None)),
        check_vma=False,
    )
```

```python
import jax
import jax.numpy as jnp
from jax import lax
from jax.experimental import pallas as pl
from jax.experimental.pallas import tpu as pltpu
from jax.sharding import Mesh, PartitionSpec as P

epsilon = 1e-06
loss_scale = 64.0
AXES = ("y", "xl", "zh", "zl", "xh", "core")
SIZES = (4, 2, 4, 4, 2, 2)
ROWS = ("zh", "zl", "xh", "core", "y", "xl")
bf16 = jnp.bfloat16
f32 = jnp.float32


def shift(value, axis, steps):
    count = lax.axis_size(axis)
    return lax.ppermute(value, axis, [(i, (i + steps) % count) for i in range(count)])


def shift_x(value, steps):
    def index(place):
        place = place % 4
        return (place % 2) * 2 + place // 2

    return lax.ppermute(value, ("xl", "xh"), [(index(i), index(i + steps)) for i in range(4)])


def swap(value):
    return lax.ppermute(value, ("xl", "core"), [(0, 0), (1, 2), (2, 1), (3, 3)])


def halves(flag, first, second, axis):
    return jnp.where(
        flag == 0,
        jnp.concatenate([first, second], axis),
        jnp.concatenate([second, first], axis),
    )


def dot(a, b, da, db):
    return lax.dot_general(a, b, (((da,), (db,)), ((), ())), preferred_element_type=f32)


def spread_to(value, axes):
    count = lax.axis_size(axes)
    many = jnp.broadcast_to(value[None], (count,) + value.shape)
    return lax.all_to_all(many, axes, split_axis=0, concat_axis=0, tiled=True)


def after(value, *others):
    return lax.optimization_barrier((value,) + others)[0]


def gather_weight(blocks, xl, core, earlier):
    count, rows, half = blocks.shape
    other = [shift_x(blocks[:2], 1), shift_x(blocks[2:], -1)]
    own_half = jnp.zeros((count, 2, rows, half), bf16)
    own_half = lax.dynamic_update_slice(own_half, blocks[:, None], (0, xl, 0, 0))
    for start, block in zip((0, 2), other):
        own_half = lax.dynamic_update_slice(own_half, block[:, None], (start, 1 - xl, 0, 0))
    own_half = after(own_half.reshape(2 * count * rows, half), *earlier)
    weight = jnp.zeros((2 * count * rows, 2 * half), bf16)
    weight = lax.dynamic_update_slice(weight, own_half, (0, core * half))
    weight = lax.dynamic_update_slice(weight, shift(own_half, "core", 1), (0, (1 - core) * half))
    return weight


def place_kernel(own, below, above, far, gain, bias, text, normed, xhat):
    rows = own.shape[1]
    lines = 32
    for index, block in enumerate((own, below, above, far)):

        def body(step, carry, index=index, block=block):
            start = pl.multiple_of(step * lines, lines)
            source, target = pl.ds(start, lines), pl.ds(index * rows + start, lines)
            text[target, :] = block[0, source, :]
            values = block[1, source, :].astype(f32)
            centered = values - jnp.mean(values, axis=1, keepdims=True)
            spread = jnp.mean(centered * centered, axis=1, keepdims=True)
            standard = centered * lax.rsqrt(spread + epsilon)
            xhat[target, :] = standard
            normed[target, :] = (standard * gain[...] + bias[...]).astype(bf16)
            return carry

        lax.fori_loop(0, rows // lines, body, 0)


def place(blocks, gain, bias):
    rows, width = blocks[0].shape[1:]
    shape = (len(blocks) * rows, width)
    return pl.pallas_call(
        place_kernel,
        out_shape=[jax.ShapeDtypeStruct(shape, t) for t in (bf16, bf16, f32)],
        in_specs=[pl.BlockSpec(memory_space=pltpu.VMEM)] * 6,
        out_specs=[pl.BlockSpec(memory_space=pltpu.VMEM)] * 3,
        compiler_params=pltpu.CompilerParams(vmem_limit_bytes=40 * 2**20),
    )(*blocks, gain.reshape(1, width), bias.reshape(1, width))


def local(
    image_features, final_norm_gain, final_norm_bias, head_weight, text_embed, log_scale, logit_bias
):
    y, xl, xh, core = (lax.axis_index(a) for a in ("y", "xl", "xh", "core"))
    scale = jnp.exp(log_scale[0])
    offset = logit_bias[0]
    own, width = image_features.shape
    half = width // 2
    block = width // 4

    weight_part = lax.dynamic_slice(head_weight, (0, core * half), (head_weight.shape[0], half))
    weight_part, text_embed, image_features = lax.optimization_barrier(
        (jnp.broadcast_to(weight_part[None], (4,) + weight_part.shape), text_embed, image_features)
    )
    weight_blocks = lax.all_to_all(weight_part, "y", split_axis=0, concat_axis=0, tiled=True)
    text_rows, feature_rows = swap(jnp.stack([text_embed, image_features], 0))

    text_values = text_rows.astype(f32)
    inv_text = lax.rsqrt(jnp.sum(text_values * text_values, axis=1, keepdims=True) + epsilon)
    text_unit = (text_values * inv_text).astype(bf16)

    pair = jnp.stack([text_unit, feature_rows], 0)
    below, above, far = shift(pair, "y", 1), shift(pair, "y", -1), shift(pair, "y", 2)
    weight = gather_weight(weight_blocks, xl, core, [below, above, far])
    text_same, normed, xhat = place([pair, below, above, far], final_norm_gain, final_norm_bias)
    text_other = shift(text_same, "core", 1)
    rows = normed.shape[0]

    projected = dot(normed, weight, 1, 0)
    inv_proj = lax.rsqrt(jnp.sum(projected * projected, axis=1, keepdims=True) + epsilon)
    image_unit = (projected * inv_proj).astype(bf16)

    def weights_of(text_rows, diagonal):
        logits = scale * dot(image_unit, text_rows, 1, 1) + offset
        return (loss_scale * (jax.nn.sigmoid(logits) - diagonal)).astype(bf16)

    weights_same = weights_of(text_same, jnp.eye(rows, dtype=f32))
    weights_other = weights_of(text_other, 0.0)
    grad_image = scale * (dot(weights_same, text_same, 1, 0) + dot(weights_other, text_other, 1, 0))
    proj_dot = jnp.sum(projected * grad_image, axis=1, keepdims=True)
    grad_proj = (
        inv_proj * grad_image - inv_proj * inv_proj * inv_proj * proj_dot * projected
    ).astype(bf16)

    normed_block = lax.dynamic_slice(normed, (0, y * block), (rows, block))
    theirs = lax.dynamic_slice(grad_proj, (0, (1 - core) * half), (rows, half))
    sent = dot(normed_block, theirs, 0, 0).astype(bf16)
    grad_proj, sent = lax.optimization_barrier((grad_proj, sent))
    mine = lax.dynamic_slice(grad_proj, (0, core * half), (rows, half))
    head = dot(normed_block, mine, 0, 0) + shift(sent, "core", 1).astype(f32)
    part = block // 4
    lanes = 128

    grad_normed = dot(grad_proj, weight, 1, 1)
    vectors = jnp.stack([jnp.sum(grad_normed * xhat, axis=0), jnp.sum(grad_normed, axis=0)], 0)
    xhat, grad_normed = xhat[:own], grad_normed[:own]
    values = feature_rows.astype(f32)
    centered = values - jnp.mean(values, axis=1, keepdims=True)
    inverse_deviation = lax.rsqrt(jnp.mean(centered * centered, axis=1, keepdims=True) + epsilon)

    lines = part // 4
    count = width // 4 // lanes
    side = vectors.astype(bf16).reshape(1, 2, 4, count, lanes)
    side = jnp.pad(side, ((0, 0), (0, 0), (0, 0), (0, lines - count), (0, 0)))
    side = jnp.broadcast_to(side, (2,) + side.shape[1:]).reshape(4, part, lanes)
    head = head.astype(bf16)
    held = after((weights_same, weights_other, image_unit), head)
    sent = jnp.concatenate([head.reshape(4, part, half), side], -1)
    received = lax.all_to_all(sent, ("xl", "xh"), split_axis=0, concat_axis=0, tiled=True)
    head = jnp.sum(received.astype(f32), axis=0).astype(bf16)

    text_part, text_theirs = (
        dot(w[:, :own], held[2], 0, 0) for w in held[:2]
    )
    grad_unit_text = text_part + shift(text_theirs, "core", 1)

    sent = head.reshape(4, lines, half + lanes)
    received = lax.all_to_all(sent, "zl", split_axis=0, concat_axis=0, tiled=True)
    sent = jnp.sum(received.astype(f32), axis=0).astype(bf16)

    grad_unit_text, grad_normed = after((grad_unit_text, grad_normed), sent)
    grad_unit_text = scale * grad_unit_text
    text_dot = jnp.sum(text_values * grad_unit_text, axis=1, keepdims=True)
    grad_text = inv_text * grad_unit_text - inv_text * inv_text * inv_text * text_dot * text_values
    scaled = grad_normed * final_norm_gain
    first_mean = jnp.mean(scaled, axis=1, keepdims=True)
    second_mean = jnp.mean(scaled * xhat, axis=1, keepdims=True)
    grad_features = inverse_deviation * (scaled - first_mean - xhat * second_mean)
    returned = swap(jnp.stack([grad_features, grad_text], 0).astype(bf16))

    received = spread_to(sent, "zh")
    sent = jnp.sum(received.astype(f32), axis=0).astype(bf16)
    mine = spread_to(sent, ("zl", "xh"))
    theirs = shift(mine, "core", 1)

    def unpack(received):
        received = received.reshape(4, 2, lines, half + lanes).transpose(1, 0, 2, 3)
        vectors = received[..., :count, half:].astype(f32).reshape(2, width)
        return received[..., :half].reshape(2 * part, half), vectors

    (head_mine, vectors_mine), (head_theirs, vectors_theirs) = unpack(mine), unpack(theirs)
    head_all = halves(core, head_mine, head_theirs, 1).astype(f32) / 64.0
    vectors = (vectors_mine + vectors_theirs) / 64.0

    return (
        returned[0].astype(f32),
        returned[1].astype(f32),
        vectors[0],
        vectors[1],
        head_all,
    )


def solution(mesh):
    fine = Mesh(mesh.devices.reshape(SIZES), AXES)
    placed = (P(ROWS, None), P(), P(), P(("y", "xl"), None), P(ROWS, None), P(), P())
    return jax.shard_map(
        local,
        mesh=fine,
        in_specs=placed,
        out_specs=(P(ROWS, None), P(ROWS, None), P(), P(), P(("y", "xl"), None)),
        check_vma=False,
    )
```

```python
import jax
import jax.numpy as jnp
from jax import lax
from jax.experimental import pallas as pl
from jax.experimental.pallas import tpu as pltpu
from jax.sharding import Mesh, PartitionSpec as P

epsilon = 1e-06
loss_scale = 64.0
AXES = ("y", "xl", "zh", "zl", "xh", "core")
SIZES = (4, 2, 4, 4, 2, 2)
ROWS = ("zh", "zl", "xh", "core", "y", "xl")
bf16 = jnp.bfloat16
f32 = jnp.float32


def shift(value, axis, steps):
    count = lax.axis_size(axis)
    return lax.ppermute(value, axis, [(i, (i + steps) % count) for i in range(count)])


def shift_x(value, steps):
    def index(place):
        place = place % 4
        return (place % 2) * 2 + place // 2

    return lax.ppermute(value, ("xl", "xh"), [(index(i), index(i + steps)) for i in range(4)])


def swap(value):
    return lax.ppermute(value, ("xl", "core"), [(0, 0), (1, 2), (2, 1), (3, 3)])


def halves(flag, first, second, axis):
    return jnp.where(
        flag == 0,
        jnp.concatenate([first, second], axis),
        jnp.concatenate([second, first], axis),
    )


def dot(a, b, da, db):
    return lax.dot_general(a, b, (((da,), (db,)), ((), ())), preferred_element_type=f32)


def spread_to(value, axes):
    count = lax.axis_size(axes)
    many = jnp.broadcast_to(value[None], (count,) + value.shape)
    return lax.all_to_all(many, axes, split_axis=0, concat_axis=0, tiled=True)


def after(value, *others):
    return lax.optimization_barrier((value,) + others)[0]


def gather_weight(blocks, xl, core, earlier):
    count, rows, half = blocks.shape
    other = [shift_x(blocks[:2], 1), shift_x(blocks[2:], -1)]
    own_half = jnp.zeros((count, 2, rows, half), bf16)
    own_half = lax.dynamic_update_slice(own_half, blocks[:, None], (0, xl, 0, 0))
    for start, block in zip((0, 2), other):
        own_half = lax.dynamic_update_slice(own_half, block[:, None], (start, 1 - xl, 0, 0))
    own_half = after(own_half.reshape(2 * count * rows, half), *earlier)
    weight = jnp.zeros((2 * count * rows, 2 * half), bf16)
    weight = lax.dynamic_update_slice(weight, own_half, (0, core * half))
    weight = lax.dynamic_update_slice(weight, shift(own_half, "core", 1), (0, (1 - core) * half))
    return weight


def place_kernel(own, below, above, far, gain, bias, text, normed, xhat):
    rows = own.shape[1]
    lines = 32
    for index, block in enumerate((own, below, above, far)):

        def body(step, carry, index=index, block=block):
            start = pl.multiple_of(step * lines, lines)
            source, target = pl.ds(start, lines), pl.ds(index * rows + start, lines)
            text[target, :] = block[0, source, :]
            values = block[1, source, :].astype(f32)
            centered = values - jnp.mean(values, axis=1, keepdims=True)
            spread = jnp.mean(centered * centered, axis=1, keepdims=True)
            standard = centered * lax.rsqrt(spread + epsilon)
            xhat[target, :] = standard
            normed[target, :] = (standard * gain[...] + bias[...]).astype(bf16)
            return carry

        lax.fori_loop(0, rows // lines, body, 0)


def place(blocks, gain, bias):
    rows, width = blocks[0].shape[1:]
    shape = (len(blocks) * rows, width)
    return pl.pallas_call(
        place_kernel,
        out_shape=[jax.ShapeDtypeStruct(shape, t) for t in (bf16, bf16, f32)],
        in_specs=[pl.BlockSpec(memory_space=pltpu.VMEM)] * 6,
        out_specs=[pl.BlockSpec(memory_space=pltpu.VMEM)] * 3,
        compiler_params=pltpu.CompilerParams(vmem_limit_bytes=40 * 2**20),
    )(*blocks, gain.reshape(1, width), bias.reshape(1, width))


def local(
    image_features, final_norm_gain, final_norm_bias, head_weight, text_embed, log_scale, logit_bias
):
    y, xl, xh, core = (lax.axis_index(a) for a in ("y", "xl", "xh", "core"))
    scale = jnp.exp(log_scale[0])
    offset = logit_bias[0]
    own, width = image_features.shape
    half = width // 2
    block = width // 4

    text_rows, feature_rows = swap(jnp.stack([text_embed, image_features], 0))
    weight_part = lax.dynamic_slice(head_weight, (0, core * half), (head_weight.shape[0], half))
    weight_blocks = spread_to(weight_part, "y")

    text_values = text_rows.astype(f32)
    inv_text = lax.rsqrt(jnp.sum(text_values * text_values, axis=1, keepdims=True) + epsilon)
    text_unit = (text_values * inv_text).astype(bf16)

    pair = jnp.stack([text_unit, feature_rows], 0)
    below, above, far = shift(pair, "y", 1), shift(pair, "y", -1), shift(pair, "y", 2)
    weight = gather_weight(weight_blocks, xl, core, [below, above, far])
    text_same, normed, xhat = place([pair, below, above, far], final_norm_gain, final_norm_bias)
    text_other = shift(text_same, "core", 1)
    rows = normed.shape[0]

    projected = dot(normed, weight, 1, 0)
    inv_proj = lax.rsqrt(jnp.sum(projected * projected, axis=1, keepdims=True) + epsilon)
    image_unit = (projected * inv_proj).astype(bf16)

    def weights_of(text_rows, diagonal):
        logits = scale * dot(image_unit, text_rows, 1, 1) + offset
        return (loss_scale * (jax.nn.sigmoid(logits) - diagonal)).astype(bf16)

    weights_same = weights_of(text_same, jnp.eye(rows, dtype=f32))
    weights_other = weights_of(text_other, 0.0)
    grad_image = scale * (dot(weights_same, text_same, 1, 0) + dot(weights_other, text_other, 1, 0))
    proj_dot = jnp.sum(projected * grad_image, axis=1, keepdims=True)
    grad_proj = (
        inv_proj * grad_image - inv_proj * inv_proj * inv_proj * proj_dot * projected
    ).astype(bf16)

    normed_block = lax.dynamic_slice(normed, (0, y * block), (rows, block))
    theirs = lax.dynamic_slice(grad_proj, (0, (1 - core) * half), (rows, half))
    sent = dot(normed_block, theirs, 0, 0).astype(bf16)
    grad_proj, sent = lax.optimization_barrier((grad_proj, sent))
    mine = lax.dynamic_slice(grad_proj, (0, core * half), (rows, half))
    head = dot(normed_block, mine, 0, 0) + shift(sent, "core", 1).astype(f32)
    part = block // 4
    lanes = 128

    grad_normed = dot(grad_proj, weight, 1, 1)
    vectors = jnp.stack([jnp.sum(grad_normed * xhat, axis=0), jnp.sum(grad_normed, axis=0)], 0)
    values = feature_rows.astype(f32)
    centered = values - jnp.mean(values, axis=1, keepdims=True)
    inverse_deviation = lax.rsqrt(jnp.mean(centered * centered, axis=1, keepdims=True) + epsilon)

    lines = part // 4
    count = width // 4 // lanes
    side = vectors.astype(bf16).reshape(1, 2, 4, count, lanes)
    side = jnp.pad(side, ((0, 0), (0, 0), (0, 0), (0, lines - count), (0, 0)))
    side = jnp.broadcast_to(side, (2,) + side.shape[1:]).reshape(4, part, lanes)
    head = head.astype(bf16)
    sent = jnp.concatenate([head.reshape(4, part, half), side], -1)
    received = lax.all_to_all(sent, ("xl", "xh"), split_axis=0, concat_axis=0, tiled=True)
    head = jnp.sum(received.astype(f32), axis=0).astype(bf16)

    sent = head.reshape(4, lines, half + lanes)
    received = lax.all_to_all(sent, "zl", split_axis=0, concat_axis=0, tiled=True)
    sent = jnp.sum(received.astype(f32), axis=0).astype(bf16)

    held = after((weights_same, weights_other, image_unit, grad_normed, xhat), sent)
    text_part, text_theirs = (dot(w[:, :own], held[2], 0, 0) for w in held[:2])
    grad_normed, xhat = held[3][:own], held[4][:own]
    grad_unit_text = text_part + shift(text_theirs, "core", 1)
    grad_unit_text = scale * grad_unit_text
    text_dot = jnp.sum(text_values * grad_unit_text, axis=1, keepdims=True)
    grad_text = inv_text * grad_unit_text - inv_text * inv_text * inv_text * text_dot * text_values
    scaled = grad_normed * final_norm_gain
    first_mean = jnp.mean(scaled, axis=1, keepdims=True)
    second_mean = jnp.mean(scaled * xhat, axis=1, keepdims=True)
    grad_features = inverse_deviation * (scaled - first_mean - xhat * second_mean)
    returned = swap(jnp.stack([grad_features, grad_text], 0).astype(bf16))

    received = spread_to(sent, "zh")
    sent = jnp.sum(received.astype(f32), axis=0).astype(bf16)
    mine = spread_to(sent, ("zl", "xh"))
    theirs = shift(mine, "core", 1)

    def unpack(received):
        received = received.reshape(4, 2, lines, half + lanes).transpose(1, 0, 2, 3)
        vectors = received[..., :count, half:].astype(f32).reshape(2, width)
        return received[..., :half].reshape(2 * part, half), vectors

    (head_mine, vectors_mine), (head_theirs, vectors_theirs) = unpack(mine), unpack(theirs)
    head_all = halves(core, head_mine, head_theirs, 1).astype(f32) / 64.0
    vectors = (vectors_mine + vectors_theirs) / 64.0

    return (
        returned[0].astype(f32),
        returned[1].astype(f32),
        vectors[0],
        vectors[1],
        head_all,
    )


def solution(mesh):
    fine = Mesh(mesh.devices.reshape(SIZES), AXES)
    placed = (P(ROWS, None), P(), P(), P(("y", "xl"), None), P(ROWS, None), P(), P())
    return jax.shard_map(
        local,
        mesh=fine,
        in_specs=placed,
        out_specs=(P(ROWS, None), P(ROWS, None), P(), P(), P(("y", "xl"), None)),
        check_vma=False,
    )
```

```python
import jax
import jax.numpy as jnp
from jax import lax
from jax.experimental import pallas as pl
from jax.experimental.pallas import tpu as pltpu
from jax.sharding import Mesh, PartitionSpec as P

epsilon = 1e-06
loss_scale = 64.0
AXES = ("y", "xl", "zh", "zl", "xh", "core")
SIZES = (4, 2, 4, 4, 2, 2)
ROWS = ("zh", "zl", "xh", "core", "y", "xl")
bf16 = jnp.bfloat16
f32 = jnp.float32


def shift(value, axis, steps):
    count = lax.axis_size(axis)
    return lax.ppermute(value, axis, [(i, (i + steps) % count) for i in range(count)])


def shift_x(value, steps):
    def index(place):
        place = place % 4
        return (place % 2) * 2 + place // 2

    return lax.ppermute(value, ("xl", "xh"), [(index(i), index(i + steps)) for i in range(4)])


def swap(value):
    return lax.ppermute(value, ("xl", "core"), [(0, 0), (1, 2), (2, 1), (3, 3)])


def halves(flag, first, second, axis):
    return jnp.where(
        flag == 0,
        jnp.concatenate([first, second], axis),
        jnp.concatenate([second, first], axis),
    )


def dot(a, b, da, db):
    return lax.dot_general(a, b, (((da,), (db,)), ((), ())), preferred_element_type=f32)


def spread_to(value, axes):
    count = lax.axis_size(axes)
    many = jnp.broadcast_to(value[None], (count,) + value.shape)
    return lax.all_to_all(many, axes, split_axis=0, concat_axis=0, tiled=True)


def after(value, *others):
    return lax.optimization_barrier((value,) + others)[0]


def gather_weight(blocks, xl, core, earlier):
    count, rows, half = blocks.shape
    other = [shift_x(blocks[:2], 1), shift_x(blocks[2:], -1)]
    own_half = jnp.zeros((count, 2, rows, half), bf16)
    own_half = lax.dynamic_update_slice(own_half, blocks[:, None], (0, xl, 0, 0))
    for start, block in zip((0, 2), other):
        own_half = lax.dynamic_update_slice(own_half, block[:, None], (start, 1 - xl, 0, 0))
    own_half = own_half.reshape(2 * count * rows, half)
    weight = jnp.zeros((2 * count * rows, 2 * half), bf16)
    weight = lax.dynamic_update_slice(weight, own_half, (0, core * half))
    own_half, weight = lax.optimization_barrier((own_half, weight, *earlier))[:2]
    weight = lax.dynamic_update_slice(weight, shift(own_half, "core", 1), (0, (1 - core) * half))
    return weight


def place_kernel(own, below, above, far, gain, bias, text, normed, xhat):
    rows = own.shape[1]
    lines = 32
    for index, block in enumerate((own, below, above, far)):

        def body(step, carry, index=index, block=block):
            start = pl.multiple_of(step * lines, lines)
            source, target = pl.ds(start, lines), pl.ds(index * rows + start, lines)
            text[target, :] = block[0, source, :]
            values = block[1, source, :].astype(f32)
            centered = values - jnp.mean(values, axis=1, keepdims=True)
            spread = jnp.mean(centered * centered, axis=1, keepdims=True)
            standard = centered * lax.rsqrt(spread + epsilon)
            xhat[target, :] = standard
            normed[target, :] = (standard * gain[...] + bias[...]).astype(bf16)
            return carry

        lax.fori_loop(0, rows // lines, body, 0)


def place(blocks, gain, bias):
    rows, width = blocks[0].shape[1:]
    shape = (len(blocks) * rows, width)
    return pl.pallas_call(
        place_kernel,
        out_shape=[jax.ShapeDtypeStruct(shape, t) for t in (bf16, bf16, f32)],
        in_specs=[pl.BlockSpec(memory_space=pltpu.VMEM)] * 6,
        out_specs=[pl.BlockSpec(memory_space=pltpu.VMEM)] * 3,
        cost_estimate=pl.CostEstimate(
            flops=40 * shape[0] * width, bytes_accessed=48 * shape[0] * width, transcendentals=shape[0]
        ),
        compiler_params=pltpu.CompilerParams(vmem_limit_bytes=40 * 2**20),
    )(*blocks, gain.reshape(1, width), bias.reshape(1, width))


def local(
    image_features, final_norm_gain, final_norm_bias, head_weight, text_embed, log_scale, logit_bias
):
    y, xl, xh, core = (lax.axis_index(a) for a in ("y", "xl", "xh", "core"))
    scale = jnp.exp(log_scale[0])
    offset = logit_bias[0]
    own, width = image_features.shape
    half = width // 2
    block = width // 4

    text_rows, feature_rows = swap(jnp.stack([text_embed, image_features], 0))
    weight_part = lax.dynamic_slice(head_weight, (0, core * half), (head_weight.shape[0], half))
    weight_blocks = spread_to(weight_part, "y")

    text_values = text_rows.astype(f32)
    inv_text = lax.rsqrt(jnp.sum(text_values * text_values, axis=1, keepdims=True) + epsilon)
    text_unit = (text_values * inv_text).astype(bf16)

    pair = jnp.stack([text_unit, feature_rows], 0)
    below, above, far = shift(pair, "y", 1), shift(pair, "y", -1), shift(pair, "y", 2)
    weight = gather_weight(weight_blocks, xl, core, [below, above])
    text_same, normed, xhat = place([pair, below, above, far], final_norm_gain, final_norm_bias)
    text_other = shift(text_same, "core", 1)
    rows = normed.shape[0]

    projected = dot(normed, weight, 1, 0)
    inv_proj = lax.rsqrt(jnp.sum(projected * projected, axis=1, keepdims=True) + epsilon)
    image_unit = (projected * inv_proj).astype(bf16)

    def weights_of(text_rows, diagonal):
        logits = scale * dot(image_unit, text_rows, 1, 1) + offset
        return (loss_scale * (jax.nn.sigmoid(logits) - diagonal)).astype(bf16)

    weights_same = weights_of(text_same, jnp.eye(rows, dtype=f32))
    weights_other = weights_of(text_other, 0.0)
    grad_image = scale * (dot(weights_same, text_same, 1, 0) + dot(weights_other, text_other, 1, 0))
    proj_dot = jnp.sum(projected * grad_image, axis=1, keepdims=True)
    grad_proj = (
        inv_proj * grad_image - inv_proj * inv_proj * inv_proj * proj_dot * projected
    ).astype(bf16)

    normed_block = lax.dynamic_slice(normed, (0, y * block), (rows, block))
    theirs = lax.dynamic_slice(grad_proj, (0, (1 - core) * half), (rows, half))
    sent = dot(normed_block, theirs, 0, 0).astype(bf16)
    grad_proj, sent = lax.optimization_barrier((grad_proj, sent))
    mine = lax.dynamic_slice(grad_proj, (0, core * half), (rows, half))
    head = dot(normed_block, mine, 0, 0) + shift(sent, "core", 1).astype(f32)
    part = block // 4
    lanes = 128

    grad_normed = dot(grad_proj, weight, 1, 1)
    vectors = jnp.stack([jnp.sum(grad_normed * xhat, axis=0), jnp.sum(grad_normed, axis=0)], 0)
    values = feature_rows.astype(f32)
    centered = values - jnp.mean(values, axis=1, keepdims=True)
    inverse_deviation = lax.rsqrt(jnp.mean(centered * centered, axis=1, keepdims=True) + epsilon)

    lines = part // 4
    count = width // 4 // lanes
    side = vectors.astype(bf16).reshape(1, 2, 4, count, lanes)
    side = jnp.pad(side, ((0, 0), (0, 0), (0, 0), (0, lines - count), (0, 0)))
    side = jnp.broadcast_to(side, (2,) + side.shape[1:]).reshape(4, part, lanes)
    head = head.astype(bf16)
    sent = jnp.concatenate([head.reshape(4, part, half), side], -1)
    received = lax.all_to_all(sent, ("xl", "xh"), split_axis=0, concat_axis=0, tiled=True)
    head = jnp.sum(received.astype(f32), axis=0).astype(bf16)

    sent = head.reshape(4, lines, half + lanes)
    received = lax.all_to_all(sent, "zl", split_axis=0, concat_axis=0, tiled=True)
    sent = jnp.sum(received.astype(f32), axis=0).astype(bf16)

    held = after((weights_same, weights_other, image_unit, grad_normed, xhat), sent)
    text_part, text_theirs = (dot(w[:, :own], held[2], 0, 0) for w in held[:2])
    grad_normed, xhat = held[3][:own], held[4][:own]
    grad_unit_text = text_part + shift(text_theirs, "core", 1)
    grad_unit_text = scale * grad_unit_text
    text_dot = jnp.sum(text_values * grad_unit_text, axis=1, keepdims=True)
    grad_text = inv_text * grad_unit_text - inv_text * inv_text * inv_text * text_dot * text_values
    scaled = grad_normed * final_norm_gain
    first_mean = jnp.mean(scaled, axis=1, keepdims=True)
    second_mean = jnp.mean(scaled * xhat, axis=1, keepdims=True)
    grad_features = inverse_deviation * (scaled - first_mean - xhat * second_mean)
    returned = swap(jnp.stack([grad_features, grad_text], 0).astype(bf16))

    received = spread_to(sent, "zh")
    sent = jnp.sum(received.astype(f32), axis=0).astype(bf16)
    mine = spread_to(sent, ("zl", "xh"))
    theirs = shift(mine, "core", 1)

    def unpack(received):
        received = received.reshape(4, 2, lines, half + lanes).transpose(1, 0, 2, 3)
        vectors = received[..., :count, half:].astype(f32).reshape(2, width)
        return received[..., :half].reshape(2 * part, half), vectors

    (head_mine, vectors_mine), (head_theirs, vectors_theirs) = unpack(mine), unpack(theirs)
    head_all = halves(core, head_mine, head_theirs, 1).astype(f32) / 64.0
    vectors = (vectors_mine + vectors_theirs) / 64.0

    return (
        returned[0].astype(f32),
        returned[1].astype(f32),
        vectors[0],
        vectors[1],
        head_all,
    )


def solution(mesh):
    fine = Mesh(mesh.devices.reshape(SIZES), AXES)
    placed = (P(ROWS, None), P(), P(), P(("y", "xl"), None), P(ROWS, None), P(), P())
    return jax.shard_map(
        local,
        mesh=fine,
        in_specs=placed,
        out_specs=(P(ROWS, None), P(ROWS, None), P(), P(), P(("y", "xl"), None)),
        check_vma=False,
    )
```

```python
import jax
import jax.numpy as jnp
from jax import lax
from jax.experimental import pallas as pl
from jax.experimental.pallas import tpu as pltpu
from jax.sharding import Mesh, PartitionSpec as P

epsilon = 1e-06
loss_scale = 64.0
AXES = ("y", "xl", "zh", "zl", "xh", "core")
SIZES = (4, 2, 4, 4, 2, 2)
ROWS = ("zh", "zl", "xh", "core", "y", "xl")
bf16 = jnp.bfloat16
f32 = jnp.float32


def shift(value, axis, steps):
    count = lax.axis_size(axis)
    return lax.ppermute(value, axis, [(i, (i + steps) % count) for i in range(count)])


def shift_x(value, steps):
    def index(place):
        place = place % 4
        return (place % 2) * 2 + place // 2

    return lax.ppermute(value, ("xl", "xh"), [(index(i), index(i + steps)) for i in range(4)])


def swap(value):
    return lax.ppermute(value, ("xl", "core"), [(0, 0), (1, 2), (2, 1), (3, 3)])


def halves(flag, first, second, axis):
    return jnp.where(
        flag == 0,
        jnp.concatenate([first, second], axis),
        jnp.concatenate([second, first], axis),
    )


def dot(a, b, da, db):
    return lax.dot_general(a, b, (((da,), (db,)), ((), ())), preferred_element_type=f32)


def spread_to(value, axes):
    count = lax.axis_size(axes)
    many = jnp.broadcast_to(value[None], (count,) + value.shape)
    return lax.all_to_all(many, axes, split_axis=0, concat_axis=0, tiled=True)


def after(value, *others):
    return lax.optimization_barrier((value,) + others)[0]


def gather_weight(blocks, xl, core, earlier):
    count, rows, half = blocks.shape
    other = [shift_x(blocks[:2], 1), shift_x(blocks[2:], -1)]
    own_half = jnp.zeros((count, 2, rows, half), bf16)
    own_half = lax.dynamic_update_slice(own_half, blocks[:, None], (0, xl, 0, 0))
    for start, block in zip((0, 2), other):
        own_half = lax.dynamic_update_slice(own_half, block[:, None], (start, 1 - xl, 0, 0))
    own_half = after(own_half.reshape(2 * count * rows, half), *earlier)
    weight = jnp.zeros((2 * count * rows, 2 * half), bf16)
    weight = lax.dynamic_update_slice(weight, own_half, (0, core * half))
    weight = lax.dynamic_update_slice(weight, shift(own_half, "core", 1), (0, (1 - core) * half))
    return weight


def place_kernel(own, below, above, far, gain, bias, text, normed, xhat):
    rows = own.shape[1]
    lines = 32
    for index, block in enumerate((own, below, above, far)):

        def body(step, carry, index=index, block=block):
            start = pl.multiple_of(step * lines, lines)
            source, target = pl.ds(start, lines), pl.ds(index * rows + start, lines)
            text[target, :] = block[0, source, :]
            values = block[1, source, :].astype(f32)
            centered = values - jnp.mean(values, axis=1, keepdims=True)
            spread = jnp.mean(centered * centered, axis=1, keepdims=True)
            standard = centered * lax.rsqrt(spread + epsilon)
            xhat[target, :] = standard
            normed[target, :] = (standard * gain[...] + bias[...]).astype(bf16)
            return carry

        lax.fori_loop(0, rows // lines, body, 0)


def place(blocks, gain, bias):
    rows, width = blocks[0].shape[1:]
    shape = (len(blocks) * rows, width)
    return pl.pallas_call(
        place_kernel,
        out_shape=[jax.ShapeDtypeStruct(shape, t) for t in (bf16, bf16, f32)],
        in_specs=[pl.BlockSpec(memory_space=pltpu.VMEM)] * 6,
        out_specs=[pl.BlockSpec(memory_space=pltpu.VMEM)] * 3,
        compiler_params=pltpu.CompilerParams(vmem_limit_bytes=40 * 2**20),
    )(*blocks, gain.reshape(1, width), bias.reshape(1, width))


def local(
    image_features, final_norm_gain, final_norm_bias, head_weight, text_embed, log_scale, logit_bias
):
    y, xl, xh, core = (lax.axis_index(a) for a in ("y", "xl", "xh", "core"))
    scale = jnp.exp(log_scale[0])
    offset = logit_bias[0]
    own, width = image_features.shape
    half = width // 2
    block = width // 4

    text_rows, feature_rows = swap(jnp.stack([text_embed, image_features], 0))
    weight_part = lax.dynamic_slice(head_weight, (0, core * half), (head_weight.shape[0], half))
    weight_blocks = spread_to(weight_part, "y")

    text_values = text_rows.astype(f32)
    inv_text = lax.rsqrt(jnp.sum(text_values * text_values, axis=1, keepdims=True) + epsilon)
    text_unit = (text_values * inv_text).astype(bf16)

    pair = jnp.stack([text_unit, feature_rows], 0)
    below, above, far = shift(pair, "y", 1), shift(pair, "y", -1), shift(pair, "y", 2)
    weight_blocks = after(weight_blocks, below, above)
    weight = gather_weight(weight_blocks, xl, core, [far])
    text_same, normed, xhat = place([pair, below, above, far], final_norm_gain, final_norm_bias)
    text_other = shift(text_same, "core", 1)
    rows = normed.shape[0]

    projected = dot(normed, weight, 1, 0)
    inv_proj = lax.rsqrt(jnp.sum(projected * projected, axis=1, keepdims=True) + epsilon)
    image_unit = (projected * inv_proj).astype(bf16)

    def weights_of(text_rows, diagonal):
        logits = scale * dot(image_unit, text_rows, 1, 1) + offset
        return (loss_scale * (jax.nn.sigmoid(logits) - diagonal)).astype(bf16)

    weights_same = weights_of(text_same, jnp.eye(rows, dtype=f32))
    weights_other = weights_of(text_other, 0.0)
    grad_image = scale * (dot(weights_same, text_same, 1, 0) + dot(weights_other, text_other, 1, 0))
    proj_dot = jnp.sum(projected * grad_image, axis=1, keepdims=True)
    grad_proj = (
        inv_proj * grad_image - inv_proj * inv_proj * inv_proj * proj_dot * projected
    ).astype(bf16)

    normed_block = lax.dynamic_slice(normed, (0, y * block), (rows, block))
    theirs = lax.dynamic_slice(grad_proj, (0, (1 - core) * half), (rows, half))
    sent = dot(normed_block, theirs, 0, 0).astype(bf16)
    grad_proj, sent = lax.optimization_barrier((grad_proj, sent))
    mine = lax.dynamic_slice(grad_proj, (0, core * half), (rows, half))
    head = dot(normed_block, mine, 0, 0) + shift(sent, "core", 1).astype(f32)
    part = block // 4
    lanes = 128

    grad_normed = dot(grad_proj, weight, 1, 1)
    vectors = jnp.stack([jnp.sum(grad_normed * xhat, axis=0), jnp.sum(grad_normed, axis=0)], 0)
    values = feature_rows.astype(f32)
    centered = values - jnp.mean(values, axis=1, keepdims=True)
    inverse_deviation = lax.rsqrt(jnp.mean(centered * centered, axis=1, keepdims=True) + epsilon)

    lines = part // 4
    count = width // 4 // lanes
    side = vectors.astype(bf16).reshape(1, 2, 4, count, lanes)
    side = jnp.pad(side, ((0, 0), (0, 0), (0, 0), (0, lines - count), (0, 0)))
    side = jnp.broadcast_to(side, (2,) + side.shape[1:]).reshape(4, part, lanes)
    head = head.astype(bf16)
    sent = jnp.concatenate([head.reshape(4, part, half), side], -1)
    received = lax.all_to_all(sent, ("xl", "xh"), split_axis=0, concat_axis=0, tiled=True)
    head = jnp.sum(received.astype(f32), axis=0).astype(bf16)

    sent = head.reshape(4, lines, half + lanes)
    received = lax.all_to_all(sent, "zl", split_axis=0, concat_axis=0, tiled=True)
    sent = jnp.sum(received.astype(f32), axis=0).astype(bf16)

    held = after((weights_same, weights_other, image_unit, grad_normed, xhat), sent)
    text_part, text_theirs = (dot(w[:, :own], held[2], 0, 0) for w in held[:2])
    grad_normed, xhat = held[3][:own], held[4][:own]
    grad_unit_text = text_part + shift(text_theirs, "core", 1)
    grad_unit_text = scale * grad_unit_text
    text_dot = jnp.sum(text_values * grad_unit_text, axis=1, keepdims=True)
    grad_text = inv_text * grad_unit_text - inv_text * inv_text * inv_text * text_dot * text_values
    scaled = grad_normed * final_norm_gain
    first_mean = jnp.mean(scaled, axis=1, keepdims=True)
    second_mean = jnp.mean(scaled * xhat, axis=1, keepdims=True)
    grad_features = inverse_deviation * (scaled - first_mean - xhat * second_mean)
    returned = swap(jnp.stack([grad_features, grad_text], 0).astype(bf16))

    received = spread_to(sent, "zh")
    sent = jnp.sum(received.astype(f32), axis=0).astype(bf16)
    mine = spread_to(sent, ("zl", "xh"))
    theirs = shift(mine, "core", 1)

    def unpack(received):
        received = received.reshape(4, 2, lines, half + lanes).transpose(1, 0, 2, 3)
        vectors = received[..., :count, half:].astype(f32).reshape(2, width)
        return received[..., :half].reshape(2 * part, half), vectors

    (head_mine, vectors_mine), (head_theirs, vectors_theirs) = unpack(mine), unpack(theirs)
    head_all = halves(core, head_mine, head_theirs, 1).astype(f32) / 64.0
    vectors = (vectors_mine + vectors_theirs) / 64.0

    return (
        returned[0].astype(f32),
        returned[1].astype(f32),
        vectors[0],
        vectors[1],
        head_all,
    )


def solution(mesh):
    fine = Mesh(mesh.devices.reshape(SIZES), AXES)
    placed = (P(ROWS, None), P(), P(), P(("y", "xl"), None), P(ROWS, None), P(), P())
    return jax.shard_map(
        local,
        mesh=fine,
        in_specs=placed,
        out_specs=(P(ROWS, None), P(ROWS, None), P(), P(), P(("y", "xl"), None)),
        check_vma=False,
    )
```

```python
import jax
import jax.numpy as jnp
from jax import lax
from jax.experimental import pallas as pl
from jax.experimental.pallas import tpu as pltpu
from jax.sharding import Mesh, PartitionSpec as P

epsilon = 1e-06
loss_scale = 64.0
AXES = ("y", "xl", "zh", "zl", "xh", "core")
SIZES = (4, 2, 4, 4, 2, 2)
ROWS = ("zh", "zl", "xh", "core", "y", "xl")
bf16 = jnp.bfloat16
f32 = jnp.float32


def shift(value, axis, steps):
    count = lax.axis_size(axis)
    return lax.ppermute(value, axis, [(i, (i + steps) % count) for i in range(count)])


def shift_x(value, steps):
    def index(place):
        place = place % 4
        return (place % 2) * 2 + place // 2

    return lax.ppermute(value, ("xl", "xh"), [(index(i), index(i + steps)) for i in range(4)])


def swap(value):
    return lax.ppermute(value, ("xl", "core"), [(0, 0), (1, 2), (2, 1), (3, 3)])


def halves(flag, first, second, axis):
    return jnp.where(
        flag == 0,
        jnp.concatenate([first, second], axis),
        jnp.concatenate([second, first], axis),
    )


def dot(a, b, da, db):
    return lax.dot_general(a, b, (((da,), (db,)), ((), ())), preferred_element_type=f32)


def spread_to(value, axes):
    count = lax.axis_size(axes)
    many = jnp.broadcast_to(value[None], (count,) + value.shape)
    return lax.all_to_all(many, axes, split_axis=0, concat_axis=0, tiled=True)


def after(value, *others):
    return lax.optimization_barrier((value,) + others)[0]


def gather_weight(blocks, xl, core, earlier):
    count, rows, half = blocks.shape
    other = [shift_x(blocks[:2], 1), shift_x(blocks[2:], -1)]
    own_half = jnp.zeros((count, 2, rows, half), bf16)
    own_half = lax.dynamic_update_slice(own_half, blocks[:, None], (0, xl, 0, 0))
    for start, block in zip((0, 2), other):
        own_half = lax.dynamic_update_slice(own_half, block[:, None], (start, 1 - xl, 0, 0))
    own_half = after(own_half.reshape(2 * count * rows, half), *earlier)
    weight = jnp.zeros((2 * count * rows, 2 * half), bf16)
    weight = lax.dynamic_update_slice(weight, own_half, (0, core * half))
    weight = lax.dynamic_update_slice(weight, shift(own_half, "core", 1), (0, (1 - core) * half))
    return weight


def swap_along(value, steps):
    pairs = [
        (4 * y + 2 * xl + core, 4 * ((y + steps) % 4) + 2 * core + xl)
        for y in range(4)
        for xl in range(2)
        for core in range(2)
    ]
    return lax.ppermute(value, ("y", "xl", "core"), pairs)


def place_kernel(own, below, above, far, gain, bias, text, normed, xhat):
    rows = own.shape[1]
    lines = 32
    for index, block in enumerate((own, below, above, far)):

        def body(step, carry, index=index, block=block):
            start = pl.multiple_of(step * lines, lines)
            source, target = pl.ds(start, lines), pl.ds(index * rows + start, lines)
            words = block[0, source, :].astype(f32)
            inverse = lax.rsqrt(jnp.sum(words * words, axis=1, keepdims=True) + epsilon)
            text[target, :] = (words * inverse).astype(bf16)
            values = block[1, source, :].astype(f32)
            centered = values - jnp.mean(values, axis=1, keepdims=True)
            spread = jnp.mean(centered * centered, axis=1, keepdims=True)
            standard = centered * lax.rsqrt(spread + epsilon)
            xhat[target, :] = standard
            normed[target, :] = (standard * gain[...] + bias[...]).astype(bf16)
            return carry

        lax.fori_loop(0, rows // lines, body, 0)


def place(blocks, gain, bias):
    rows, width = blocks[0].shape[1:]
    shape = (len(blocks) * rows, width)
    return pl.pallas_call(
        place_kernel,
        out_shape=[jax.ShapeDtypeStruct(shape, t) for t in (bf16, bf16, f32)],
        in_specs=[pl.BlockSpec(memory_space=pltpu.VMEM)] * 6,
        out_specs=[pl.BlockSpec(memory_space=pltpu.VMEM)] * 3,
        compiler_params=pltpu.CompilerParams(vmem_limit_bytes=40 * 2**20),
    )(*blocks, gain.reshape(1, width), bias.reshape(1, width))


def local(
    image_features, final_norm_gain, final_norm_bias, head_weight, text_embed, log_scale, logit_bias
):
    y, xl, xh, core = (lax.axis_index(a) for a in ("y", "xl", "xh", "core"))
    scale = jnp.exp(log_scale[0])
    offset = logit_bias[0]
    own, width = image_features.shape
    half = width // 2
    block = width // 4

    weight_part = lax.dynamic_slice(head_weight, (0, core * half), (head_weight.shape[0], half))
    weight_blocks = spread_to(weight_part, "y")

    pair = jnp.stack([text_embed, image_features], 0)
    mine, below, above, far = (swap_along(pair, step) for step in (0, 1, -1, 2))
    weight_blocks = after(weight_blocks, mine, below, above)
    weight = gather_weight(weight_blocks, xl, core, [far])
    text_rows, feature_rows = mine
    text_values = text_rows.astype(f32)
    inv_text = lax.rsqrt(jnp.sum(text_values * text_values, axis=1, keepdims=True) + epsilon)
    text_same, normed, xhat = place([mine, below, above, far], final_norm_gain, final_norm_bias)
    text_other = shift(text_same, "core", 1)
    rows = normed.shape[0]

    projected = dot(normed, weight, 1, 0)
    inv_proj = lax.rsqrt(jnp.sum(projected * projected, axis=1, keepdims=True) + epsilon)
    image_unit = (projected * inv_proj).astype(bf16)

    def weights_of(text_rows, diagonal):
        logits = scale * dot(image_unit, text_rows, 1, 1) + offset
        return (loss_scale * (jax.nn.sigmoid(logits) - diagonal)).astype(bf16)

    weights_same = weights_of(text_same, jnp.eye(rows, dtype=f32))
    weights_other = weights_of(text_other, 0.0)
    grad_image = scale * (dot(weights_same, text_same, 1, 0) + dot(weights_other, text_other, 1, 0))
    proj_dot = jnp.sum(projected * grad_image, axis=1, keepdims=True)
    grad_proj = (
        inv_proj * grad_image - inv_proj * inv_proj * inv_proj * proj_dot * projected
    ).astype(bf16)

    normed_block = lax.dynamic_slice(normed, (0, y * block), (rows, block))
    theirs = lax.dynamic_slice(grad_proj, (0, (1 - core) * half), (rows, half))
    sent = dot(normed_block, theirs, 0, 0).astype(bf16)
    grad_proj, sent = lax.optimization_barrier((grad_proj, sent))
    kept = lax.dynamic_slice(grad_proj, (0, core * half), (rows, half))
    head = dot(normed_block, kept, 0, 0) + shift(sent, "core", 1).astype(f32)
    part = block // 4
    lanes = 128

    grad_normed = dot(grad_proj, weight, 1, 1)
    vectors = jnp.stack([jnp.sum(grad_normed * xhat, axis=0), jnp.sum(grad_normed, axis=0)], 0)
    values = feature_rows.astype(f32)
    centered = values - jnp.mean(values, axis=1, keepdims=True)
    inverse_deviation = lax.rsqrt(jnp.mean(centered * centered, axis=1, keepdims=True) + epsilon)

    lines = part // 4
    count = width // 4 // lanes
    side = vectors.astype(bf16).reshape(1, 2, 4, count, lanes)
    side = jnp.pad(side, ((0, 0), (0, 0), (0, 0), (0, lines - count), (0, 0)))
    side = jnp.broadcast_to(side, (2,) + side.shape[1:]).reshape(4, part, lanes)
    head = head.astype(bf16)
    sent = jnp.concatenate([head.reshape(4, part, half), side], -1)
    received = lax.all_to_all(sent, ("xl", "xh"), split_axis=0, concat_axis=0, tiled=True)
    head = jnp.sum(received.astype(f32), axis=0).astype(bf16)

    sent = head.reshape(4, lines, half + lanes)
    received = lax.all_to_all(sent, "zl", split_axis=0, concat_axis=0, tiled=True)
    sent = jnp.sum(received.astype(f32), axis=0).astype(bf16)

    held = after((weights_same, weights_other, image_unit, grad_normed, xhat), sent)
    text_part, text_theirs = (dot(w[:, :own], held[2], 0, 0) for w in held[:2])
    grad_normed, xhat = held[3][:own], held[4][:own]
    grad_unit_text = text_part + shift(text_theirs, "core", 1)
    grad_unit_text = scale * grad_unit_text
    text_dot = jnp.sum(text_values * grad_unit_text, axis=1, keepdims=True)
    grad_text = inv_text * grad_unit_text - inv_text * inv_text * inv_text * text_dot * text_values
    scaled = grad_normed * final_norm_gain
    first_mean = jnp.mean(scaled, axis=1, keepdims=True)
    second_mean = jnp.mean(scaled * xhat, axis=1, keepdims=True)
    grad_features = inverse_deviation * (scaled - first_mean - xhat * second_mean)
    returned = swap(jnp.stack([grad_features, grad_text], 0).astype(bf16))

    received = spread_to(sent, "zh")
    sent = jnp.sum(received.astype(f32), axis=0).astype(bf16)
    mine = spread_to(sent, ("zl", "xh"))
    theirs = shift(mine, "core", 1)

    def unpack(received):
        received = received.reshape(4, 2, lines, half + lanes).transpose(1, 0, 2, 3)
        vectors = received[..., :count, half:].astype(f32).reshape(2, width)
        return received[..., :half].reshape(2 * part, half), vectors

    (head_mine, vectors_mine), (head_theirs, vectors_theirs) = unpack(mine), unpack(theirs)
    head_all = halves(core, head_mine, head_theirs, 1).astype(f32) / 64.0
    vectors = (vectors_mine + vectors_theirs) / 64.0

    return (
        returned[0].astype(f32),
        returned[1].astype(f32),
        vectors[0],
        vectors[1],
        head_all,
    )


def solution(mesh):
    fine = Mesh(mesh.devices.reshape(SIZES), AXES)
    placed = (P(ROWS, None), P(), P(), P(("y", "xl"), None), P(ROWS, None), P(), P())
    return jax.shard_map(
        local,
        mesh=fine,
        in_specs=placed,
        out_specs=(P(ROWS, None), P(ROWS, None), P(), P(), P(("y", "xl"), None)),
        check_vma=False,
    )
```

```python
import jax
import jax.numpy as jnp
from jax import lax
from jax.experimental import pallas as pl
from jax.experimental.pallas import tpu as pltpu
from jax.sharding import Mesh, PartitionSpec as P

epsilon = 1e-06
loss_scale = 64.0
AXES = ("y", "xl", "zh", "zl", "xh", "core")
SIZES = (4, 2, 4, 4, 2, 2)
ROWS = ("zh", "zl", "xh", "core", "y", "xl")
bf16 = jnp.bfloat16
f32 = jnp.float32


def shift(value, axis, steps):
    count = lax.axis_size(axis)
    return lax.ppermute(value, axis, [(i, (i + steps) % count) for i in range(count)])


def swap(value):
    return lax.ppermute(value, ("xl", "core"), [(0, 0), (1, 2), (2, 1), (3, 3)])


def halves(flag, first, second, axis):
    return jnp.where(
        flag == 0,
        jnp.concatenate([first, second], axis),
        jnp.concatenate([second, first], axis),
    )


def dot(a, b, da, db):
    return lax.dot_general(a, b, (((da,), (db,)), ((), ())), preferred_element_type=f32)


def spread_to(value, axes):
    count = lax.axis_size(axes)
    many = jnp.broadcast_to(value[None], (count,) + value.shape)
    return lax.all_to_all(many, axes, split_axis=0, concat_axis=0, tiled=True)


def after(value, *others):
    return lax.optimization_barrier((value,) + others)[0]


def place_kernel(own, below, above, far, gain, bias, text, normed, xhat):
    rows = own.shape[1]
    lines = 32
    for index, block in enumerate((own, below, above, far)):

        def body(step, carry, index=index, block=block):
            start = pl.multiple_of(step * lines, lines)
            source, target = pl.ds(start, lines), pl.ds(index * rows + start, lines)
            text[target, :] = block[0, source, :]
            values = block[1, source, :].astype(f32)
            centered = values - jnp.mean(values, axis=1, keepdims=True)
            spread = jnp.mean(centered * centered, axis=1, keepdims=True)
            standard = centered * lax.rsqrt(spread + epsilon)
            xhat[target, :] = standard
            normed[target, :] = (standard * gain[...] + bias[...]).astype(bf16)
            return carry

        lax.fori_loop(0, rows // lines, body, 0)


def place(blocks, gain, bias):
    rows, width = blocks[0].shape[1:]
    shape = (len(blocks) * rows, width)
    return pl.pallas_call(
        place_kernel,
        out_shape=[jax.ShapeDtypeStruct(shape, t) for t in (bf16, bf16, f32)],
        in_specs=[pl.BlockSpec(memory_space=pltpu.VMEM)] * 6,
        out_specs=[pl.BlockSpec(memory_space=pltpu.VMEM)] * 3,
        compiler_params=pltpu.CompilerParams(vmem_limit_bytes=40 * 2**20),
    )(*blocks, gain.reshape(1, width), bias.reshape(1, width))


def local(
    image_features, final_norm_gain, final_norm_bias, head_weight, text_embed, log_scale, logit_bias
):
    y, xl, xh, core = (lax.axis_index(a) for a in ("y", "xl", "xh", "core"))
    scale = jnp.exp(log_scale[0])
    offset = logit_bias[0]
    own, width = image_features.shape
    half = width // 2
    block = width // 4

    text_rows, feature_rows = swap(jnp.stack([text_embed, image_features], 0))
    weight_part = lax.dynamic_slice(head_weight, (0, core * half), (head_weight.shape[0], half))
    weight_half = spread_to(weight_part, ("y", "xl")).reshape(width, half)

    text_values = text_rows.astype(f32)
    inv_text = lax.rsqrt(jnp.sum(text_values * text_values, axis=1, keepdims=True) + epsilon)
    text_unit = (text_values * inv_text).astype(bf16)

    pair = jnp.stack([text_unit, feature_rows], 0)
    below, above, far = shift(pair, "y", 1), shift(pair, "y", -1), shift(pair, "y", 2)
    weight = jnp.zeros((width, width), bf16)
    weight = lax.dynamic_update_slice(weight, weight_half, (0, core * half))
    weight_half = shift(after(weight_half, below, above, far), "core", 1)
    weight = lax.dynamic_update_slice(weight, weight_half, (0, (1 - core) * half))
    text_same, normed, xhat = place([pair, below, above, far], final_norm_gain, final_norm_bias)
    text_other = shift(text_same, "core", 1)
    rows = normed.shape[0]

    projected = dot(normed, weight, 1, 0)
    inv_proj = lax.rsqrt(jnp.sum(projected * projected, axis=1, keepdims=True) + epsilon)
    image_unit = (projected * inv_proj).astype(bf16)

    def weights_of(text_rows, diagonal):
        logits = scale * dot(image_unit, text_rows, 1, 1) + offset
        return (loss_scale * (jax.nn.sigmoid(logits) - diagonal)).astype(bf16)

    weights_same = weights_of(text_same, jnp.eye(rows, dtype=f32))
    weights_other = weights_of(text_other, 0.0)
    grad_image = scale * (dot(weights_same, text_same, 1, 0) + dot(weights_other, text_other, 1, 0))
    proj_dot = jnp.sum(projected * grad_image, axis=1, keepdims=True)
    grad_proj = (
        inv_proj * grad_image - inv_proj * inv_proj * inv_proj * proj_dot * projected
    ).astype(bf16)

    normed_block = lax.dynamic_slice(normed, (0, y * block), (rows, block))
    theirs = lax.dynamic_slice(grad_proj, (0, (1 - core) * half), (rows, half))
    sent = dot(normed_block, theirs, 0, 0).astype(bf16)
    grad_proj, sent = lax.optimization_barrier((grad_proj, sent))
    mine = lax.dynamic_slice(grad_proj, (0, core * half), (rows, half))
    head = dot(normed_block, mine, 0, 0) + shift(sent, "core", 1).astype(f32)
    part = block // 4
    lanes = 128

    grad_normed = dot(grad_proj, weight, 1, 1)
    vectors = jnp.stack([jnp.sum(grad_normed * xhat, axis=0), jnp.sum(grad_normed, axis=0)], 0)
    values = feature_rows.astype(f32)
    centered = values - jnp.mean(values, axis=1, keepdims=True)
    inverse_deviation = lax.rsqrt(jnp.mean(centered * centered, axis=1, keepdims=True) + epsilon)

    lines = part // 4
    count = width // 4 // lanes
    side = vectors.astype(bf16).reshape(1, 2, 4, count, lanes)
    side = jnp.pad(side, ((0, 0), (0, 0), (0, 0), (0, lines - count), (0, 0)))
    side = jnp.broadcast_to(side, (2,) + side.shape[1:]).reshape(4, part, lanes)
    head = head.astype(bf16)
    sent = jnp.concatenate([head.reshape(4, part, half), side], -1)
    received = lax.all_to_all(sent, ("xl", "xh"), split_axis=0, concat_axis=0, tiled=True)
    head = jnp.sum(received.astype(f32), axis=0).astype(bf16)

    sent = head.reshape(4, lines, half + lanes)
    received = lax.all_to_all(sent, "zl", split_axis=0, concat_axis=0, tiled=True)
    sent = jnp.sum(received.astype(f32), axis=0).astype(bf16)

    held = after((weights_same, weights_other, image_unit, grad_normed, xhat), sent)
    text_part, text_theirs = (dot(w[:, :own], held[2], 0, 0) for w in held[:2])
    grad_normed, xhat = held[3][:own], held[4][:own]
    grad_unit_text = text_part + shift(text_theirs, "core", 1)
    grad_unit_text = scale * grad_unit_text
    text_dot = jnp.sum(text_values * grad_unit_text, axis=1, keepdims=True)
    grad_text = inv_text * grad_unit_text - inv_text * inv_text * inv_text * text_dot * text_values
    scaled = grad_normed * final_norm_gain
    first_mean = jnp.mean(scaled, axis=1, keepdims=True)
    second_mean = jnp.mean(scaled * xhat, axis=1, keepdims=True)
    grad_features = inverse_deviation * (scaled - first_mean - xhat * second_mean)
    returned = swap(jnp.stack([grad_features, grad_text], 0).astype(bf16))

    received = spread_to(sent, "zh")
    sent = jnp.sum(received.astype(f32), axis=0).astype(bf16)
    mine = spread_to(sent, ("zl", "xh"))
    theirs = shift(mine, "core", 1)

    def unpack(received):
        received = received.reshape(4, 2, lines, half + lanes).transpose(1, 0, 2, 3)
        vectors = received[..., :count, half:].astype(f32).reshape(2, width)
        return received[..., :half].reshape(2 * part, half), vectors

    (head_mine, vectors_mine), (head_theirs, vectors_theirs) = unpack(mine), unpack(theirs)
    head_all = halves(core, head_mine, head_theirs, 1).astype(f32) / 64.0
    vectors = (vectors_mine + vectors_theirs) / 64.0

    return (
        returned[0].astype(f32),
        returned[1].astype(f32),
        vectors[0],
        vectors[1],
        head_all,
    )


def solution(mesh):
    fine = Mesh(mesh.devices.reshape(SIZES), AXES)
    placed = (P(ROWS, None), P(), P(), P(("y", "xl"), None), P(ROWS, None), P(), P())
    return jax.shard_map(
        local,
        mesh=fine,
        in_specs=placed,
        out_specs=(P(ROWS, None), P(ROWS, None), P(), P(), P(("y", "xl"), None)),
        check_vma=False,
    )
```
